512 devices in a mesh: dp: 512 (over x, z, y, core).
Axes of the slice: x: 4, y: 8, z: 8, core: 2. Of those that a mesh axis runs over, the one named last changes fastest.
Arguments:
- student_image_vectors: bfloat16 [196608, 768], P('dp'), may hold values from -6 to 6
- teacher_emb: bfloat16 [196608, 768], P('dp'), may hold values from -6 to 6
- text_emb: bfloat16 [196608, 768], P('dp'), may hold values from -6 to 6
- species: int32 [196608], P('dp'), may hold values from 0 to 999
Outputs:
- grad_student: float32 [196608, 768], P('dp')
- grad_text: float32 [196608, 768], P('dp')
- loss_rows: float32 [196608], P('dp')
The draws below stay inside these ranges and needn't reach their ends.
Inputs may be any that keep to these rules, and one draw needn't show every extreme that they name: species ids; pairs with equal ids count as positives.
All inputs are finite; a program needn't handle non-finite values.
Results may differ from the reference program's by a relative error of at most 0.0015.
Values may be sent and summed in bfloat16 or wider, within the bound.
No kernel may reach another device: no remote copies, remote signals or barrier semaphores. Data moves between devices by JAX's collectives and lax.ppermute only.
A program may use at most 64 MiB of HBM per device.

```python
import math
import jax
import jax.numpy as jnp
import numpy as np
from jax import lax

EMBED_WIDTH = 768
ROWS = 384
HOPS = 3
BATCH = 196608
N_DP = 512


def with_ends(entries, rng, smallest, largest):
    shape = entries.shape
    spot = [jax.random.randint(jax.random.fold_in(rng, axis), (), 0, shape[axis]) for axis in range(len(shape))]
    entries = entries.at[tuple(spot)].set(smallest)
    longest = shape.index(max(shape))
    spot[longest] = (spot[longest] + 1) % shape[longest]
    return entries.at[tuple(spot)].set(largest)


def level_of(stream_key, dims, shards, smallest, largest):
    factor_of, own = 1.0, jax.random.fold_in(stream_key, 6)
    for position, blocks in shards:
        draws = jnp.exp(jax.random.uniform(jax.random.fold_in(own, position), (blocks,), jnp.float32, smallest / len(shards), largest / len(shards)))
        factor_of = factor_of * jnp.repeat(draws, dims[position] // blocks).reshape([-1 if axis == position else 1 for axis in range(len(dims))])
    return factor_of


def rank_table(count, skew):
    loads = [(1 << 20) // math.isqrt(rank ** skew) + 1 for rank in range(1, count + 1)]
    width = 1 + sum(loads) // (1 << 30)
    return np.cumsum(np.array([max(1, weight // width) for weight in loads]))


def ranked_ids(rng, shape, count, skew):
    table = rank_table(count, skew)
    pick = jax.random.randint(jax.random.fold_in(rng, 1), shape, 0, int(table[count - 1]))
    standing = jnp.searchsorted(jnp.asarray(table, jnp.int32), pick, side="right")
    return jax.random.permutation(jax.random.fold_in(rng, 2), count)[standing].astype(jnp.int32)


def gaussian(key, extent, scale, reach, split=(), dtype=jnp.bfloat16):
    level = level_of(key, extent, split, -0.22, 0.18) if split else 1.0
    array = jax.random.normal(key, extent, jnp.float32) * scale * level
    return jnp.minimum(jnp.maximum(array, -reach), reach).astype(dtype)


def setup_inputs(seed: int = 0) -> dict:
    streams_of = jax.random.split(jax.random.key(seed), 5)
    return {
        "student_image_vectors": gaussian(streams_of[0], (BATCH, EMBED_WIDTH), 1.0, 6.0, ((0, 512),)),
        "teacher_emb": gaussian(streams_of[1], (BATCH, EMBED_WIDTH), 1.0, 6.0, ((0, 512),)),
        "text_emb": gaussian(streams_of[2], (BATCH, EMBED_WIDTH), 1.0, 6.0, ((0, 512),)),
        "species": with_ends(ranked_ids(streams_of[3], (BATCH,), 1000, 2), jax.random.fold_in(streams_of[3], 3), 0, 999).astype(jnp.int32),
    }


SOFTMAX_TEMP_VALUE = 4.0
LOGIT_BIAS = -3.0

def reference(student_image_vectors, teacher_emb, text_emb, species):
    logit_scale_multiplier = SOFTMAX_TEMP_VALUE / math.sqrt(EMBED_WIDTH)
    student = student_image_vectors.astype(jnp.float32).reshape(N_DP, ROWS, EMBED_WIDTH)
    teacher = teacher_emb.astype(jnp.float32).reshape(N_DP, ROWS, EMBED_WIDTH)
    texts = text_emb.astype(jnp.float32).reshape(N_DP, ROWS, EMBED_WIDTH)
    labels = species.reshape(N_DP, ROWS)
    grad_student = jnp.zeros((N_DP, ROWS, EMBED_WIDTH), jnp.float32)
    grad_text = jnp.zeros((N_DP, ROWS, EMBED_WIDTH), jnp.float32)
    loss_sum = jnp.zeros((N_DP, ROWS), jnp.float32)
    for offset in range(-HOPS, HOPS + 1):
        caption_block = jnp.roll(texts, -offset, axis=0)
        text_labels = jnp.roll(labels, -offset, axis=0)
        student_pair_logit = jnp.einsum('prd,pcd->prc', student, caption_block) * logit_scale_multiplier + LOGIT_BIAS
        teacher_logit = jnp.einsum('prd,pcd->prc', teacher, caption_block) * logit_scale_multiplier + LOGIT_BIAS
        positive = (labels[:, :, None] == text_labels[:, None, :]).astype(jnp.float32)
        target = 0.5 * positive + 0.5 * jax.nn.sigmoid(teacher_logit)
        loss_sum = loss_sum + lax.optimization_barrier(jnp.sum(jax.nn.softplus(student_pair_logit) - target * student_pair_logit, axis=2))
        slope = (jax.nn.sigmoid(student_pair_logit) - target).astype(jnp.bfloat16)
        slope = lax.optimization_barrier(slope).astype(jnp.float32)
        grad_student = grad_student + jnp.einsum('prc,pcd->prd', slope, caption_block) * logit_scale_multiplier
        term = jnp.einsum('prc,prd->pcd', slope, student) * logit_scale_multiplier
        grad_text = grad_text + jnp.roll(term, offset, axis=0)
    loss_rows = loss_sum / float((2 * HOPS + 1) * ROWS)
    return (grad_student.reshape(BATCH, EMBED_WIDTH), grad_text.reshape(BATCH, EMBED_WIDTH), loss_rows.reshape(BATCH))
```

```python
import jax
import jax.numpy as jnp
from jax import lax
from jax.experimental import pallas as pl
from jax.experimental.pallas import tpu as pltpu
from jax.sharding import PartitionSpec as P

SOFTMAX_TEMP_VALUE = 4.0
LOGIT_BIAS = -3.0
WINDOW = 7
DIGIT = 32.0
LANES = 128
EXTRA = 16

BF16 = jnp.bfloat16
F32 = jnp.float32


def moved(value, even, odd):
    length = lax.axis_size("dp")
    return lax.ppermute(
        value, "dp", [(i, (i + (odd if i % 2 else even)) % length) for i in range(length)]
    )


def within(value):
    return moved(value, 1, -1)


def across(value):
    return moved(value, -1, 1)


def onward(value):
    return moved(value, 2, -2)


def back(value):
    return moved(value, -2, 2)


def call(body, out_shape, flops, *args):
    in_bytes = sum(a.size * a.dtype.itemsize for a in args)
    out_bytes = sum(o.size * o.dtype.itemsize for o in out_shape)
    return pl.pallas_call(
        body,
        out_shape=out_shape,
        in_specs=[pl.BlockSpec(memory_space=pltpu.VMEM)] * len(args),
        out_specs=[pl.BlockSpec(memory_space=pltpu.VMEM)] * len(out_shape),
        compiler_params=pltpu.CompilerParams(vmem_limit_bytes=40 * 1024 * 1024),
        cost_estimate=pl.CostEstimate(
            flops=flops, bytes_accessed=in_bytes + out_bytes, transcendentals=0
        ),
    )(*args)


def digits(species_ref):
    ids = species_ref[...].astype(F32)
    high = jnp.floor(ids / DIGIT)
    low = ids - high * DIGIT
    rows = species_ref.shape[1]
    place = lax.broadcasted_iota(jnp.int32, (EXTRA, rows), 0)
    return jnp.where(place == 0, high, jnp.where(place == 1, low, 0.0)).astype(BF16)


def pack_text(text_ref, species_ref, out_ref):
    rows, width = text_ref.shape
    out_ref[:rows, :] = text_ref[...]
    out_ref[rows:, :rows] = digits(species_ref)
    out_ref[rows:, rows:] = jnp.zeros((EXTRA, width - rows), BF16)


def pack_images(student_ref, teacher_ref, species_ref, out_ref):
    rows, width = student_ref.shape
    out_ref[:rows, :] = student_ref[...]
    out_ref[rows : 2 * rows, :] = teacher_ref[...]
    out_ref[2 * rows :, :rows] = digits(species_ref)
    out_ref[2 * rows :, rows:] = jnp.zeros((EXTRA, width - rows), BF16)


def ids_of(ref, rows, start):
    digit = ref[start : start + EXTRA, :rows].astype(F32)
    return digit[0:1, :] * DIGIT + digit[1:2, :]


def pair(student, teacher, ids, text, text_ids):
    rows, width = student.shape
    half_scale = 0.5 * SOFTMAX_TEMP_VALUE / float(width) ** 0.5
    contract = (((1,), (1,)), ((), ()))
    half_z = (
        lax.dot_general(student, text, contract, preferred_element_type=F32) * half_scale
        + 0.5 * LOGIT_BIAS
    )
    half_w = (
        lax.dot_general(teacher, text, contract, preferred_element_type=F32) * half_scale
        + 0.5 * LOGIT_BIAS
    )
    column = jnp.transpose(jnp.broadcast_to(ids, (LANES, rows)))
    column = jnp.concatenate([column] * (rows // LANES), axis=1)
    shift = jnp.where(column == text_ids, 0.75, 0.25)
    target = 0.25 * jnp.tanh(half_w) + shift
    tanh_z = jnp.tanh(half_z)
    slope = (0.5 * tanh_z + 0.5) - target
    z = half_z + half_z
    loss = (jnp.maximum(z, 0.0) - target * z) - jnp.log(0.5 * jnp.abs(tanh_z) + 0.5)
    folded = sum(loss[:, k : k + LANES] for k in range(0, rows, LANES))
    return slope.astype(BF16), folded


def text_term(slope, student):
    return lax.dot_general(slope, student, (((0,), (0,)), ((), ())), preferred_element_type=F32)


def two_blocks(first, images_ref, other_ref, text_ref, *refs):
    if first:
        own_out, other_out, term_ref = refs
    else:
        own_in, other_in, own_out, other_out, term_ref = refs
    rows, width = term_ref.shape
    text = text_ref[:rows, :]
    text_ids = ids_of(text_ref, rows, rows)
    term = None
    for block, (ref, out) in enumerate(((images_ref, own_out), (other_ref, other_out))):
        student = ref[:rows, :]
        slope, folded = pair(
            student, ref[rows : 2 * rows, :], ids_of(ref, rows, 2 * rows), text, text_ids
        )
        grad = jnp.dot(slope, text, preferred_element_type=F32)
        if not first:
            was = (own_in, other_in)[block]
            grad = grad + was[:, :width]
            folded = folded + was[:, width:]
        out[:, :width] = grad
        out[:, width:] = folded
        part = text_term(slope, student)
        term = part if term is None else term + part
    term_ref[...] = term.astype(term_ref.dtype)


def one_block(images_ref, text_ref, own_in, own_out, term_ref):
    rows, width = term_ref.shape
    text = text_ref[:rows, :]
    student = images_ref[:rows, :]
    slope, folded = pair(
        student,
        images_ref[rows : 2 * rows, :],
        ids_of(images_ref, rows, 2 * rows),
        text,
        ids_of(text_ref, rows, rows),
    )
    own_out[:, :width] = own_in[:, :width] + jnp.dot(slope, text, preferred_element_type=F32)
    own_out[:, width:] = own_in[:, width:] + folded
    term_ref[...] = text_term(slope, student).astype(term_ref.dtype)


def add_far(near_ref, far_ref, out_ref):
    out_ref[...] = (near_ref[...] + far_ref[...].astype(F32)).astype(out_ref.dtype)


def finish_images(own_ref, other_ref, grad_ref, loss_ref):
    rows, width = grad_ref.shape
    scale = SOFTMAX_TEMP_VALUE / float(width) ** 0.5
    grad_ref[...] = (own_ref[:, :width] + other_ref[:, :width]) * scale
    folded = jnp.transpose(own_ref[:, width:] + other_ref[:, width:])
    loss_ref[...] = jnp.sum(folded, axis=0, keepdims=True) / float(WINDOW * rows)


def finish_text(own_ref, after_ref, before_ref, out_ref):
    scale = SOFTMAX_TEMP_VALUE / float(out_ref.shape[1]) ** 0.5
    total = own_ref[...] + after_ref[...].astype(F32) + before_ref[...].astype(F32)
    out_ref[...] = total * scale


def shards(student_image_vectors, teacher_emb, text_emb, species):
    rows, width = text_emb.shape
    dot = 2 * rows * rows * width
    ids = species.reshape(1, rows)

    def spec(n, m, dtype):
        return jax.ShapeDtypeStruct((n, m), dtype)

    sums = spec(rows, width + LANES, F32)
    (text,) = call(pack_text, [spec(rows + EXTRA, width, BF16)], 0, text_emb, ids)
    near = across(text)
    (images,) = call(
        pack_images,
        [spec(2 * rows + EXTRA, width, BF16)],
        0,
        student_image_vectors,
        teacher_emb,
        ids,
    )
    other = within(images)
    second = onward(text)
    far = onward(near)

    own_sum, other_sum, own_term = call(
        lambda *refs: two_blocks(True, *refs),
        [sums, sums, spec(rows, width, F32)],
        8 * dot,
        images,
        other,
        text,
    )
    own_sum, other_sum, near_term = call(
        lambda *refs: two_blocks(False, *refs),
        [sums, sums, spec(rows, width, F32)],
        8 * dot,
        images,
        other,
        near,
        own_sum,
        other_sum,
    )
    own_sum, other_sum, second_term = call(
        lambda *refs: two_blocks(False, *refs),
        [sums, sums, spec(rows, width, BF16)],
        8 * dot,
        images,
        other,
        second,
        own_sum,
        other_sum,
    )
    second_back = back(second_term)
    other_back = within(other_sum)
    own_sum, far_term = call(
        one_block, [sums, spec(rows, width, BF16)], 4 * dot, images, far, own_sum
    )
    far_back = back(far_term)
    (near_total,) = call(add_far, [spec(rows, width, BF16)], 0, near_term, far_back)
    near_back = across(near_total)
    grad_student, loss = call(
        finish_images, [spec(rows, width, F32), spec(1, rows, F32)], 0, own_sum, other_back
    )
    (grad_text,) = call(
        finish_text, [spec(rows, width, F32)], 0, own_term, second_back, near_back
    )
    return grad_student, grad_text, loss.reshape(rows)


def solution(mesh):
    return jax.shard_map(
        shards,
        mesh=mesh,
        in_specs=(P("dp", None), P("dp", None), P("dp", None), P("dp")),
        out_specs=(P("dp", None), P("dp", None), P("dp")),
        check_vma=False,
    )
```

```python
import jax
import jax.numpy as jnp
from jax import lax
from jax.experimental import pallas as pl
from jax.experimental.pallas import tpu as pltpu
from jax.sharding import PartitionSpec as P

SOFTMAX_TEMP_VALUE = 4.0
LOGIT_BIAS = -3.0
WINDOW = 7
DIGIT = 32.0
LANES = 128
EXTRA = 16

BF16 = jnp.bfloat16
F32 = jnp.float32


def moved(value, even, odd):
    length = lax.axis_size("dp")
    return lax.ppermute(
        value, "dp", [(i, (i + (odd if i % 2 else even)) % length) for i in range(length)]
    )


def within(value):
    return moved(value, 1, -1)


def across(value):
    return moved(value, -1, 1)


def onward(value):
    return moved(value, 2, -2)


def back(value):
    return moved(value, -2, 2)


def call(body, out_shape, flops, *args, after=()):
    count = len(args)

    def ordered(*refs):
        body(*refs[:count], *refs[count + len(after) :])

    in_bytes = sum(a.size * a.dtype.itemsize for a in args)
    out_bytes = sum(o.size * o.dtype.itemsize for o in out_shape)
    return pl.pallas_call(
        ordered,
        out_shape=out_shape,
        in_specs=[pl.BlockSpec(memory_space=pltpu.VMEM)] * count
        + [pl.BlockSpec(memory_space=pl.ANY)] * len(after),
        out_specs=[pl.BlockSpec(memory_space=pltpu.VMEM)] * len(out_shape),
        compiler_params=pltpu.CompilerParams(vmem_limit_bytes=40 * 1024 * 1024),
        cost_estimate=pl.CostEstimate(
            flops=flops, bytes_accessed=in_bytes + out_bytes, transcendentals=0
        ),
    )(*args, *after)


def digits(species_ref):
    rows = species_ref.shape[0]
    ids = species_ref[...].reshape(1, rows).astype(F32)
    high = jnp.floor(ids / DIGIT)
    low = ids - high * DIGIT
    place = lax.broadcasted_iota(jnp.int32, (EXTRA, rows), 0)
    return jnp.where(place == 0, high, jnp.where(place == 1, low, 0.0)).astype(BF16)


def put_digits(species_ref, out_ref, start):
    rows, width = species_ref.shape[0], out_ref.shape[1]
    out_ref[start:, :rows] = digits(species_ref)
    out_ref[start:, rows:] = jnp.zeros((EXTRA, width - rows), BF16)


def pack_text(text_ref, species_ref, out_ref):
    rows = text_ref.shape[0]
    out_ref[:rows, :] = text_ref[...]
    put_digits(species_ref, out_ref, rows)


def pack_images(student_ref, teacher_ref, species_ref, out_ref):
    rows = student_ref.shape[0]
    out_ref[:rows, :] = student_ref[...]
    out_ref[rows : 2 * rows, :] = teacher_ref[...]
    put_digits(species_ref, out_ref, 2 * rows)


def ids_of(ref, rows, start):
    digit = ref[start : start + EXTRA, :rows].astype(F32)
    return digit[0:1, :] * DIGIT + digit[1:2, :]


def pair(student, teacher, ids, text, text_ids):
    rows, width = student.shape
    half_scale = 0.5 * SOFTMAX_TEMP_VALUE / float(width) ** 0.5
    contract = (((1,), (1,)), ((), ()))
    half_z = (
        lax.dot_general(student, text, contract, preferred_element_type=F32) * half_scale
        + 0.5 * LOGIT_BIAS
    )
    half_w = (
        lax.dot_general(teacher, text, contract, preferred_element_type=F32) * half_scale
        + 0.5 * LOGIT_BIAS
    )
    column = jnp.transpose(jnp.broadcast_to(ids, (LANES, rows)))
    column = jnp.concatenate([column] * (rows // LANES), axis=1)
    shift = jnp.where(column == text_ids, 0.75, 0.25)
    target = 0.25 * jnp.tanh(half_w) + shift
    tanh_z = jnp.tanh(half_z)
    slope = (0.5 * tanh_z + 0.5) - target
    z = half_z + half_z
    loss = (jnp.maximum(z, 0.0) - target * z) - jnp.log(0.5 * jnp.abs(tanh_z) + 0.5)
    folded = sum(loss[:, k : k + LANES] for k in range(0, rows, LANES))
    return slope.astype(BF16), folded


def text_term(slope, student):
    return lax.dot_general(slope, student, (((0,), (0,)), ((), ())), preferred_element_type=F32)


def packed_images(ref, rows):
    return ref.at[:rows, :], ref.at[rows : 2 * rows, :], ids_of(ref, rows, 2 * rows)


def add_block(images_ref, text_ref, was_ref, sums_ref):
    rows = sums_ref.shape[0]
    width = text_ref.shape[1]
    student_ref, teacher_ref, ids = packed_images(images_ref, rows)
    text = text_ref[:rows, :]
    student = student_ref[...]
    slope, folded = pair(student, teacher_ref[...], ids, text, ids_of(text_ref, rows, rows))
    grad = jnp.dot(slope, text, preferred_element_type=F32)
    if was_ref is not None:
        grad = grad + was_ref[:, :width]
        folded = folded + was_ref[:, width:]
    sums_ref[:, :width] = grad.astype(sums_ref.dtype)
    sums_ref[:, width:] = folded.astype(sums_ref.dtype)
    return text_term(slope, student)


def own_first(own_ref, text_ref, own_out, term_ref):
    term_ref[...] = add_block(own_ref, text_ref, None, own_out)


def own_next(own_ref, text_ref, own_in, own_out, term_ref):
    term_ref[...] = add_block(own_ref, text_ref, own_in, own_out)


def other_two(other_ref, text_ref, near_ref, own_in, near_in, other_out, own_out, near_out):
    own_out[...] = own_in[...] + add_block(other_ref, text_ref, None, other_out)
    near_out[...] = near_in[...] + add_block(other_ref, near_ref, other_out, other_out)


def both(own_ref, other_ref, text_ref, own_in, other_in, own_out, other_out, term_ref):
    term = add_block(own_ref, text_ref, own_in, own_out)
    term = term + add_block(other_ref, text_ref, other_in, other_out)
    term_ref[...] = term.astype(term_ref.dtype)


def ahead_last(ahead_ref, text_ref, term_in, ahead_out, term_ref):
    term = term_in[...] + add_block(ahead_ref, text_ref, None, ahead_out)
    term_ref[...] = term.astype(term_ref.dtype)


def gather(own_sum, other_back, own_term, second_back, sum_ref, term_ref):
    sum_ref[...] = own_sum[...] + other_back[...]
    term_ref[...] = own_term[...] + second_back[...].astype(F32)


def finish_images(own_ref, ahead_ref, grad_ref, loss_ref):
    rows, width = grad_ref.shape
    scale = SOFTMAX_TEMP_VALUE / float(width) ** 0.5
    total = own_ref[...] + ahead_ref[...].astype(F32)
    grad_ref[...] = total[:, :width] * scale
    folded = jnp.transpose(total[:, width:])
    loss_ref[...] = jnp.sum(folded, axis=0, keepdims=True) / float(WINDOW * rows)


def finish_text(own_ref, near_ref, out_ref):
    scale = SOFTMAX_TEMP_VALUE / float(out_ref.shape[1]) ** 0.5
    out_ref[...] = (own_ref[...] + near_ref[...].astype(F32)) * scale


def shards(student_image_vectors, teacher_emb, text_emb, species):
    rows, width = text_emb.shape
    dot = 2 * rows * rows * width

    def spec(n, m, dtype):
        return jax.ShapeDtypeStruct((n, m), dtype)

    sums = spec(rows, width + LANES, F32)
    term = spec(rows, width, F32)
    sent = spec(rows, width, BF16)
    packed = spec(rows + EXTRA, width, BF16)
    (text,) = call(pack_text, [packed], 0, text_emb, species)
    near = across(text)
    (images,) = call(
        pack_images,
        [spec(2 * rows + EXTRA, width, BF16)],
        0,
        student_image_vectors,
        teacher_emb,
        species,
        after=(text,),
    )
    other = within(images)
    ahead = back(images)
    second = onward(text)
    own_sum, own_term = call(own_first, [sums, term], 4 * dot, images, text)
    own_sum, near_term = call(own_next, [sums, term], 4 * dot, images, near, own_sum)
    other_sum, own_term, near_term = call(
        other_two, [sums, term, term], 8 * dot, other, text, near, own_term, near_term
    )
    ahead_sum, near_term = call(
        ahead_last,
        [spec(rows, width + LANES, BF16), sent],
        4 * dot,
        ahead,
        near,
        near_term,
    )
    near_back = across(near_term)
    ahead_back = onward(ahead_sum)
    own_sum, other_sum, second_term = call(
        both, [sums, sums, sent], 8 * dot, images, other, second, own_sum, other_sum
    )
    second_back = back(second_term)
    other_back = within(other_sum)
    own_sum, own_term = call(
        gather, [sums, term], 16 * dot, own_sum, other_back, own_term, second_back
    )
    grad_student, loss = call(
        finish_images,
        [spec(rows, width, F32), spec(1, rows, F32)],
        0,
        own_sum,
        ahead_back,
    )
    loss = loss.reshape(rows)
    (grad_text,) = call(finish_text, [term], 0, own_term, near_back, after=(loss,))
    return grad_student, grad_text, loss


def solution(mesh):
    return jax.shard_map(
        shards,
        mesh=mesh,
        in_specs=(P("dp", None), P("dp", None), P("dp", None), P("dp")),
        out_specs=(P("dp", None), P("dp", None), P("dp")),
        check_vma=False,
    )
```

```python
import jax
import jax.numpy as jnp
from jax import lax
from jax.experimental import pallas as pl
from jax.experimental.pallas import tpu as pltpu
from jax.sharding import PartitionSpec as P

SOFTMAX_TEMP_VALUE = 4.0
LOGIT_BIAS = -3.0
WINDOW = 7
DIGIT = 32.0
LANES = 128
EXTRA = 16

BF16 = jnp.bfloat16
F32 = jnp.float32


def moved(value, even, odd):
    length = lax.axis_size("dp")
    return lax.ppermute(
        value, "dp", [(i, (i + (odd if i % 2 else even)) % length) for i in range(length)]
    )


def within(value):
    return moved(value, 1, -1)


def across(value):
    return moved(value, -1, 1)


def onward(value):
    return moved(value, 2, -2)


def back(value):
    return moved(value, -2, 2)


def call(body, out_shape, flops, *args, after=()):
    count = len(args)

    def ordered(*refs):
        body(*refs[:count], *refs[count + len(after) :])

    in_bytes = sum(a.size * a.dtype.itemsize for a in args)
    out_bytes = sum(o.size * o.dtype.itemsize for o in out_shape)
    return pl.pallas_call(
        ordered,
        out_shape=out_shape,
        in_specs=[pl.BlockSpec(memory_space=pltpu.VMEM)] * count
        + [pl.BlockSpec(memory_space=pl.ANY)] * len(after),
        out_specs=[pl.BlockSpec(memory_space=pltpu.VMEM)] * len(out_shape),
        compiler_params=pltpu.CompilerParams(vmem_limit_bytes=40 * 1024 * 1024),
        cost_estimate=pl.CostEstimate(
            flops=flops, bytes_accessed=in_bytes + out_bytes, transcendentals=0
        ),
    )(*args, *after)


def spread(first, second):
    tiles = [
        row[:, k : k + LANES] for row in (first, second) for k in range(0, row.shape[1], LANES)
    ]
    place = lax.broadcasted_iota(jnp.int32, (EXTRA, LANES), 0)
    out = jnp.zeros((EXTRA, LANES), F32)
    for k, tile in enumerate(tiles):
        out = jnp.where(place == k, tile, out)
    return out.astype(BF16)


def gathered(ref, start, rows):
    tiles = ref[start:, :].astype(F32)
    count = rows // LANES
    first = jnp.concatenate([tiles[k : k + 1, :] for k in range(count)], axis=1)
    second = jnp.concatenate([tiles[k : k + 1, :] for k in range(count, 2 * count)], axis=1)
    return first, second


def digits(species):
    ids = species.reshape(1, species.shape[0]).astype(F32)
    high = jnp.floor(ids / DIGIT)
    return spread(high, ids - high * DIGIT)


def ids_of(ref, rows):
    high, low = gathered(ref, ref.shape[0] - EXTRA, rows)
    return high * DIGIT + low


def put(out_ref, start, value):
    rows = value.shape[0]
    for k in range(value.shape[1] // LANES):
        out_ref[start + k * rows : start + (k + 1) * rows, :] = value[:, k * LANES : (k + 1) * LANES]


def taken(ref, start, rows, width):
    count = width // LANES
    tiles = [ref[start + k * rows : start + (k + 1) * rows, :] for k in range(count)]
    return jnp.concatenate(tiles, axis=1)


def pack_text(text_ref, species_ref, out_ref):
    put(out_ref, 0, text_ref[...])
    out_ref[out_ref.shape[0] - EXTRA :, :] = digits(species_ref[...])


def pack_images(student_ref, teacher_ref, species_ref, out_ref):
    rows, width = student_ref.shape
    put(out_ref, 0, student_ref[...])
    put(out_ref, rows * width // LANES, teacher_ref[...])
    out_ref[out_ref.shape[0] - EXTRA :, :] = digits(species_ref[...])


def pair(student, teacher, ids, text, text_ids):
    rows, width = student.shape
    half_scale = 0.5 * SOFTMAX_TEMP_VALUE / float(width) ** 0.5
    contract = (((1,), (1,)), ((), ()))
    half_z = (
        lax.dot_general(student, text, contract, preferred_element_type=F32) * half_scale
        + 0.5 * LOGIT_BIAS
    )
    half_w = (
        lax.dot_general(teacher, text, contract, preferred_element_type=F32) * half_scale
        + 0.5 * LOGIT_BIAS
    )
    column = jnp.transpose(jnp.broadcast_to(ids, (LANES, rows)))
    column = jnp.concatenate([column] * (rows // LANES), axis=1)
    shift = jnp.where(column == text_ids, 0.75, 0.25)
    target = 0.25 * jnp.tanh(half_w) + shift
    tanh_z = jnp.tanh(half_z)
    slope = (0.5 * tanh_z + 0.5) - target
    z = half_z + half_z
    loss = (jnp.maximum(z, 0.0) - target * z) - jnp.log(0.5 * jnp.abs(tanh_z) + 0.5)
    folded = sum(loss[:, k : k + LANES] for k in range(0, rows, LANES))
    return slope.astype(BF16), folded


def text_term(slope, student):
    return lax.dot_general(slope, student, (((0,), (0,)), ((), ())), preferred_element_type=F32)


def block(images_ref, text_ref, rows):
    width = (text_ref.shape[0] - EXTRA) * LANES // rows
    text = taken(text_ref, 0, rows, width)
    student = taken(images_ref, 0, rows, width)
    teacher = taken(images_ref, rows * width // LANES, rows, width)
    slope, folded = pair(student, teacher, ids_of(images_ref, rows), text, ids_of(text_ref, rows))
    return jnp.dot(slope, text, preferred_element_type=F32), folded, text_term(slope, student)


def own_first(own_ref, text_ref, sums_ref, term_ref):
    rows, width = term_ref.shape
    sums_ref[:, :width], sums_ref[:, width:], term_ref[...] = block(own_ref, text_ref, rows)


def own_next(own_ref, text_ref, sums_in, sums_ref, term_ref):
    rows, width = term_ref.shape
    grad, folded, term_ref[...] = block(own_ref, text_ref, rows)
    sums_ref[:, :width] = sums_in[:, :width] + grad
    sums_ref[:, width:] = sums_in[:, width:] + folded


def other_all(
    other_ref,
    text_ref,
    near_ref,
    second_ref,
    own_in,
    near_in,
    second_in,
    sums_ref,
    own_out,
    near_out,
    second_out,
):
    rows, width = own_in.shape
    texts = (
        (second_ref, second_in, second_out),
        (near_ref, near_in, near_out),
        (text_ref, own_in, own_out),
    )
    for count, (ref, term_in, term_out) in enumerate(texts):
        grad, folded, term = block(other_ref, ref, rows)
        term_out[...] = (term_in[...] + term).astype(term_out.dtype)
        if count:
            grad = sums_ref[:, :width] + grad
            folded = sums_ref[:, width:] + folded
        sums_ref[:, :width] = grad
        sums_ref[:, width:] = folded


def loss_row(folded):
    return jnp.sum(jnp.transpose(folded), axis=0, keepdims=True)


def ahead_last(ahead_ref, text_ref, term_in, ahead_out, term_ref):
    rows, width = term_ref.shape
    grad, folded, term = block(ahead_ref, text_ref, rows)
    term_ref[...] = (term_in[...] + term).astype(term_ref.dtype)
    put(ahead_out, 0, grad.astype(BF16))
    loss = loss_row(folded)
    high = loss.astype(BF16).astype(F32)
    ahead_out[ahead_out.shape[0] - EXTRA :, :] = spread(high, loss - high)


def gather_text(own_ref, second_ref, term_ref):
    term_ref[...] = own_ref[...] + second_ref[...].astype(F32)


def gather_images(own_ref, ahead_ref, sums_ref, loss_ref):
    rows, width = own_ref.shape[0], own_ref.shape[1] - LANES
    sums_ref[...] = own_ref[:, :width] + taken(ahead_ref, 0, rows, width).astype(F32)
    high, low = gathered(ahead_ref, ahead_ref.shape[0] - EXTRA, rows)
    loss_ref[...] = loss_row(own_ref[:, width:]) + high + low


def finish_images(sums_in, loss_in, other_ref, grad_ref, loss_ref, done_ref):
    rows, width = grad_ref.shape
    scale = SOFTMAX_TEMP_VALUE / float(width) ** 0.5
    grad_ref[...] = (sums_in[...] + other_ref[:, :width]) * scale
    loss = loss_in[...] + loss_row(other_ref[:, width:])
    loss_ref[...] = (loss / float(WINDOW * rows)).reshape(rows)
    done_ref[...] = jnp.zeros_like(done_ref)


def finish_text(own_ref, near_ref, out_ref):
    scale = SOFTMAX_TEMP_VALUE / float(out_ref.shape[1]) ** 0.5
    out_ref[...] = (own_ref[...] + near_ref[...].astype(F32)) * scale


def shards(student_image_vectors, teacher_emb, text_emb, species):
    rows, width = text_emb.shape
    dot = 2 * rows * rows * width

    def spec(n, m, dtype):
        return jax.ShapeDtypeStruct((n, m), dtype)

    sums = spec(rows, width + LANES, F32)
    term = spec(rows, width, F32)
    sent = spec(rows, width, BF16)
    packed = spec(rows * width // LANES + EXTRA, LANES, BF16)
    (text,) = call(pack_text, [packed], 0, text_emb, species)
    near = across(text)
    second = onward(text)
    (images,) = call(
        pack_images,
        [spec(2 * rows * width // LANES + EXTRA, LANES, BF16)],
        0,
        student_image_vectors,
        teacher_emb,
        species,
        after=(text,),
    )
    ahead = back(images)
    other = within(images)
    own_sum, own_term = call(own_first, [sums, term], 4 * dot, images, text)
    own_sum, near_term = call(own_next, [sums, term], 32 * dot, images, near, own_sum)
    own_sum, second_term = call(own_next, [sums, term], 32 * dot, images, second, own_sum)
    other_sum, own_term, near_term, second_term = call(
        other_all,
        [sums, term, term, sent],
        12 * dot,
        other,
        text,
        near,
        second,
        own_term,
        near_term,
        second_term,
    )
    second_back = back(second_term)
    other_back = within(other_sum)
    ahead_sum, near_term = call(
        ahead_last, [packed, sent], 4 * dot, ahead, near, near_term
    )
    near_back = across(near_term)
    ahead_back = onward(ahead_sum)
    (own_term,) = call(gather_text, [term], 64 * dot, own_term, second_back)
    own_sum, loss = call(
        gather_images, [term, spec(1, rows, F32)], 32 * dot, own_sum, ahead_back, after=(own_term,)
    )
    grad_student, loss, done = call(
        finish_images,
        [term, jax.ShapeDtypeStruct((rows,), F32), spec(8, LANES, F32)],
        0,
        own_sum,
        loss,
        other_back,
    )
    (grad_text,) = call(finish_text, [term], 0, own_term, near_back, after=(done,))
    return grad_student, grad_text, loss


def solution(mesh):
    return jax.shard_map(
        shards,
        mesh=mesh,
        in_specs=(P("dp", None), P("dp", None), P("dp", None), P("dp")),
        out_specs=(P("dp", None), P("dp", None), P("dp")),
        check_vma=False,
    )
```

```python
import jax
import jax.numpy as jnp
from jax import lax
from jax.experimental import pallas as pl
from jax.experimental.pallas import tpu as pltpu
from jax.sharding import PartitionSpec as P

SOFTMAX_TEMP_VALUE = 4.0
LOGIT_BIAS = -3.0
WINDOW = 7
DIGIT = 32.0
LANES = 128
EXTRA = 16

BF16 = jnp.bfloat16
F32 = jnp.float32


def moved(value, even, odd):
    length = lax.axis_size("dp")
    return lax.ppermute(
        value, "dp", [(i, (i + (odd if i % 2 else even)) % length) for i in range(length)]
    )


def within(value):
    return moved(value, 1, -1)


def across(value):
    return moved(value, -1, 1)


def onward(value):
    return moved(value, 2, -2)


def back(value):
    return moved(value, -2, 2)


def call(body, out_shape, flops, *args, after=()):
    count = len(args)

    def ordered(*refs):
        body(*refs[:count], *refs[count + len(after) :])

    in_bytes = sum(a.size * a.dtype.itemsize for a in args)
    out_bytes = sum(o.size * o.dtype.itemsize for o in out_shape)
    return pl.pallas_call(
        ordered,
        out_shape=out_shape,
        in_specs=[pl.BlockSpec(memory_space=pltpu.VMEM)] * count
        + [pl.BlockSpec(memory_space=pl.ANY)] * len(after),
        out_specs=[pl.BlockSpec(memory_space=pltpu.VMEM)] * len(out_shape),
        compiler_params=pltpu.CompilerParams(vmem_limit_bytes=40 * 1024 * 1024),
        cost_estimate=pl.CostEstimate(
            flops=flops, bytes_accessed=in_bytes + out_bytes, transcendentals=0
        ),
    )(*args, *after)


def spread(first, second):
    tiles = [
        row[:, k : k + LANES] for row in (first, second) for k in range(0, row.shape[1], LANES)
    ]
    place = lax.broadcasted_iota(jnp.int32, (EXTRA, LANES), 0)
    out = jnp.zeros((EXTRA, LANES), F32)
    for k, tile in enumerate(tiles):
        out = jnp.where(place == k, tile, out)
    return out.astype(BF16)


def gathered(ref, start, rows):
    tiles = ref[start:, :].astype(F32)
    count = rows // LANES
    first = jnp.concatenate([tiles[k : k + 1, :] for k in range(count)], axis=1)
    second = jnp.concatenate([tiles[k : k + 1, :] for k in range(count, 2 * count)], axis=1)
    return first, second


def digits(species):
    ids = species.reshape(1, species.shape[0]).astype(F32)
    high = jnp.floor(ids / DIGIT)
    return spread(high, ids - high * DIGIT)


def ids_of(ref, rows):
    high, low = gathered(ref, ref.shape[0] - EXTRA, rows)
    return high * DIGIT + low


def put(out_ref, start, value):
    rows = value.shape[0]
    for k in range(value.shape[1] // LANES):
        out_ref[start + k * rows : start + (k + 1) * rows, :] = value[:, k * LANES : (k + 1) * LANES]


def taken(ref, start, rows, width):
    count = width // LANES
    tiles = [ref[start + k * rows : start + (k + 1) * rows, :] for k in range(count)]
    return jnp.concatenate(tiles, axis=1)


def pack_text(text_ref, species_ref, out_ref):
    put(out_ref, 0, text_ref[...])
    out_ref[out_ref.shape[0] - EXTRA :, :] = digits(species_ref[...])


def pack_images(student_ref, teacher_ref, species_ref, out_ref, teacher_out):
    rows, width = student_ref.shape
    ids = digits(species_ref[...])
    put(out_ref, 0, student_ref[...])
    put(out_ref, rows * width // LANES, teacher_ref[...])
    out_ref[out_ref.shape[0] - EXTRA :, :] = ids
    put(teacher_out, 0, teacher_ref[...])
    teacher_out[teacher_out.shape[0] - EXTRA :, :] = ids


def pair(student, teacher, ids, text, text_ids):
    rows, width = student.shape
    half_scale = 0.5 * SOFTMAX_TEMP_VALUE / float(width) ** 0.5
    contract = (((1,), (1,)), ((), ()))
    half_z = (
        lax.dot_general(student, text, contract, preferred_element_type=F32) * half_scale
        + 0.5 * LOGIT_BIAS
    )
    half_w = (
        lax.dot_general(teacher, text, contract, preferred_element_type=F32) * half_scale
        + 0.5 * LOGIT_BIAS
    )
    column = jnp.transpose(jnp.broadcast_to(ids, (LANES, rows)))
    column = jnp.concatenate([column] * (rows // LANES), axis=1)
    shift = jnp.where(column == text_ids, 0.75, 0.25)
    target = 0.25 * jnp.tanh(half_w) + shift
    tanh_z = jnp.tanh(half_z)
    slope = (0.5 * tanh_z + 0.5) - target
    z = half_z + half_z
    loss = (jnp.maximum(z, 0.0) - target * z) - jnp.log(0.5 * jnp.abs(tanh_z) + 0.5)
    folded = sum(loss[:, k : k + LANES] for k in range(0, rows, LANES))
    return slope.astype(BF16), folded


def text_term(slope, student):
    return lax.dot_general(slope, student, (((0,), (0,)), ((), ())), preferred_element_type=F32)


def unpacked(ref, rows):
    width = (ref.shape[0] - EXTRA) * LANES // rows
    return taken(ref, 0, rows, width), ids_of(ref, rows)


def both_images(ref, rows):
    size = (ref.shape[0] - EXTRA) // 2
    width = size * LANES // rows
    return taken(ref, 0, rows, width), taken(ref, size, rows, width), ids_of(ref, rows)


def block(images, texts):
    student, teacher, ids = images
    slope, folded = pair(student, teacher, ids, *texts)
    grad = jnp.dot(slope, texts[0], preferred_element_type=F32)
    return grad, folded, text_term(slope, student)


def add_to(sums_ref, sums_in, grad, folded):
    width = grad.shape[1]
    sums_ref[:, :width] = sums_in[:, :width] + grad
    sums_ref[:, width:] = sums_in[:, width:] + folded


def own_first(own_ref, text_ref, sums_ref, term_ref):
    rows, width = term_ref.shape
    images = both_images(own_ref, rows)
    sums_ref[:, :width], sums_ref[:, width:], term_ref[...] = block(images, unpacked(text_ref, rows))


def own_second(own_ref, text_ref, sums_in, sums_ref, term_ref):
    rows = term_ref.shape[0]
    grad, folded, term_ref[...] = block(both_images(own_ref, rows), unpacked(text_ref, rows))
    add_to(sums_ref, sums_in, grad, folded)


def other_second(other_ref, text_ref, term_in, sums_ref, term_ref):
    rows, width = term_ref.shape
    grad, folded, term = block(both_images(other_ref, rows), unpacked(text_ref, rows))
    sums_ref[:, :width] = grad
    sums_ref[:, width:] = folded
    term_ref[...] = (term_in[...] + term).astype(term_ref.dtype)


def near_and_text(
    own_ref,
    other_ref,
    text_ref,
    near_ref,
    own_in,
    other_in,
    term_in,
    own_out,
    other_out,
    near_term,
    own_term,
):
    rows = term_in.shape[0]
    near = unpacked(near_ref, rows)
    grad, folded, term = block(both_images(own_ref, rows), near)
    add_to(own_out, own_in, grad, folded)
    other = both_images(other_ref, rows)
    grad, folded, more = block(other, near)
    near_term[...] = term + more
    add_to(other_out, other_in, grad, folded)
    grad, folded, term = block(other, unpacked(text_ref, rows))
    own_term[...] = term_in[...] + term
    add_to(other_out, other_out, grad, folded)


def loss_row(folded):
    return jnp.sum(jnp.transpose(folded), axis=0, keepdims=True)


def ahead_last(student_ref, teacher_ref, near_ref, term_in, ahead_out, term_ref):
    rows = term_ref.shape[0]
    images = (student_ref[...], *unpacked(teacher_ref, rows))
    grad, folded, term = block(images, unpacked(near_ref, rows))
    term_ref[...] = (term_in[...] + term).astype(term_ref.dtype)
    put(ahead_out, 0, grad.astype(BF16))
    loss = loss_row(folded)
    high = loss.astype(BF16).astype(F32)
    ahead_out[ahead_out.shape[0] - EXTRA :, :] = spread(high, loss - high)


def gather_text(own_ref, second_ref, term_ref):
    term_ref[...] = own_ref[...] + second_ref[...].astype(F32)


def gather_images(own_ref, ahead_ref, sums_ref, loss_ref):
    rows, width = own_ref.shape[0], own_ref.shape[1] - LANES
    sums_ref[...] = own_ref[:, :width] + taken(ahead_ref, 0, rows, width).astype(F32)
    high, low = gathered(ahead_ref, ahead_ref.shape[0] - EXTRA, rows)
    loss_ref[...] = loss_row(own_ref[:, width:]) + high + low


def finish_images(sums_in, loss_in, other_ref, grad_ref, loss_ref, done_ref):
    rows, width = grad_ref.shape
    scale = SOFTMAX_TEMP_VALUE / float(width) ** 0.5
    grad_ref[...] = (sums_in[...] + other_ref[:, :width]) * scale
    loss = loss_in[...] + loss_row(other_ref[:, width:])
    loss_ref[...] = (loss / float(WINDOW * rows)).reshape(rows)
    done_ref[...] = jnp.zeros_like(done_ref)


def finish_text(own_ref, near_ref, out_ref):
    scale = SOFTMAX_TEMP_VALUE / float(out_ref.shape[1]) ** 0.5
    out_ref[...] = (own_ref[...] + near_ref[...].astype(F32)) * scale


def shards(student_image_vectors, teacher_emb, text_emb, species):
    rows, width = text_emb.shape
    dot = 2 * rows * rows * width

    def spec(n, m, dtype):
        return jax.ShapeDtypeStruct((n, m), dtype)

    sums = spec(rows, width + LANES, F32)
    term = spec(rows, width, F32)
    sent = spec(rows, width, BF16)
    packed = spec(rows * width // LANES + EXTRA, LANES, BF16)
    ahead_student = back(student_image_vectors)
    (text,) = call(pack_text, [packed], 0, text_emb, species)
    second = onward(text)
    near = across(text)
    images, teacher = call(
        pack_images,
        [spec(2 * rows * width // LANES + EXTRA, LANES, BF16), packed],
        0,
        student_image_vectors,
        teacher_emb,
        species,
        after=(text,),
    )
    other = within(images)
    ahead_teacher = back(teacher)
    own_sum, own_term = call(
        own_first, [sums, term], 64 * dot, images, text, after=(ahead_student,)
    )
    own_sum, second_term = call(own_second, [sums, term], 16 * dot, images, second, own_sum)
    other_sum, second_term = call(
        other_second, [sums, sent], 16 * dot, other, second, second_term
    )
    second_back = back(second_term)
    own_sum, other_sum, near_term, own_term = call(
        near_and_text,
        [sums, sums, term, term],
        4 * dot,
        images,
        other,
        text,
        near,
        own_sum,
        other_sum,
        own_term,
    )
    other_back = within(other_sum)
    ahead_sum, near_term = call(
        ahead_last, [packed, sent], 4 * dot, ahead_student, ahead_teacher, near, near_term
    )
    near_back = across(near_term)
    ahead_back = onward(ahead_sum)
    (own_term,) = call(gather_text, [term], 64 * dot, own_term, second_back)
    own_sum, loss = call(
        gather_images, [term, spec(1, rows, F32)], 32 * dot, own_sum, ahead_back, after=(own_term,)
    )
    grad_student, loss, done = call(
        finish_images,
        [term, jax.ShapeDtypeStruct((rows,), F32), spec(8, LANES, F32)],
        0,
        own_sum,
        loss,
        other_back,
    )
    (grad_text,) = call(finish_text, [term], 0, own_term, near_back, after=(done,))
    return grad_student, grad_text, loss


def solution(mesh):
    return jax.shard_map(
        shards,
        mesh=mesh,
        in_specs=(P("dp", None), P("dp", None), P("dp", None), P("dp")),
        out_specs=(P("dp", None), P("dp", None), P("dp")),
        check_vma=False,
    )
```

```python
import jax
import jax.numpy as jnp
from jax import lax
from jax.experimental import pallas as pl
from jax.experimental.pallas import tpu as pltpu
from jax.sharding import PartitionSpec as P

SOFTMAX_TEMP_VALUE = 4.0
LOGIT_BIAS = -3.0
WINDOW = 7
DIGIT = 32.0
LANES = 128
EXTRA = 16

BF16 = jnp.bfloat16
F32 = jnp.float32


def moved(value, even, odd):
    length = lax.axis_size("dp")
    return lax.ppermute(
        value, "dp", [(i, (i + (odd if i % 2 else even)) % length) for i in range(length)]
    )


def within(value):
    return moved(value, 1, -1)


def across(value):
    return moved(value, -1, 1)


def onward(value):
    return moved(value, 2, -2)


def back(value):
    return moved(value, -2, 2)


def call(body, out_shape, flops, *args, after=()):
    count = len(args)

    def ordered(*refs):
        body(*refs[:count], *refs[count + len(after) :])

    in_bytes = sum(a.size * a.dtype.itemsize for a in args)
    out_bytes = sum(o.size * o.dtype.itemsize for o in out_shape)
    return pl.pallas_call(
        ordered,
        out_shape=out_shape,
        in_specs=[pl.BlockSpec(memory_space=pltpu.VMEM)] * count
        + [pl.BlockSpec(memory_space=pl.ANY)] * len(after),
        out_specs=[pl.BlockSpec(memory_space=pltpu.VMEM)] * len(out_shape),
        compiler_params=pltpu.CompilerParams(vmem_limit_bytes=40 * 1024 * 1024),
        cost_estimate=pl.CostEstimate(
            flops=flops, bytes_accessed=in_bytes + out_bytes, transcendentals=0
        ),
    )(*args, *after)


def spread(first, second):
    tiles = [
        row[:, k : k + LANES] for row in (first, second) for k in range(0, row.shape[1], LANES)
    ]
    place = lax.broadcasted_iota(jnp.int32, (EXTRA, LANES), 0)
    out = jnp.zeros((EXTRA, LANES), F32)
    for k, tile in enumerate(tiles):
        out = jnp.where(place == k, tile, out)
    return out.astype(BF16)


def gathered(ref, start, rows):
    tiles = ref[start:, :].astype(F32)
    count = rows // LANES
    first = jnp.concatenate([tiles[k : k + 1, :] for k in range(count)], axis=1)
    second = jnp.concatenate([tiles[k : k + 1, :] for k in range(count, 2 * count)], axis=1)
    return first, second


def digits(species):
    ids = species.reshape(1, species.shape[0]).astype(F32)
    high = jnp.floor(ids / DIGIT)
    return spread(high, ids - high * DIGIT)


def ids_of(ref, rows):
    high, low = gathered(ref, ref.shape[0] - EXTRA, rows)
    return high * DIGIT + low


def put(out_ref, start, value):
    rows = value.shape[0]
    for k in range(value.shape[1] // LANES):
        out_ref[start + k * rows : start + (k + 1) * rows, :] = value[:, k * LANES : (k + 1) * LANES]


def taken(ref, start, rows, width):
    count = width // LANES
    tiles = [ref[start + k * rows : start + (k + 1) * rows, :] for k in range(count)]
    return jnp.concatenate(tiles, axis=1)


def pack_text(text_ref, species_ref, out_ref):
    put(out_ref, 0, text_ref[...])
    out_ref[out_ref.shape[0] - EXTRA :, :] = digits(species_ref[...])


def pack_images(student_ref, teacher_ref, species_ref, out_ref, teacher_out):
    rows, width = student_ref.shape
    ids = digits(species_ref[...])
    put(out_ref, 0, student_ref[...])
    put(out_ref, rows * width // LANES, teacher_ref[...])
    out_ref[out_ref.shape[0] - EXTRA :, :] = ids
    put(teacher_out, 0, teacher_ref[...])
    teacher_out[teacher_out.shape[0] - EXTRA :, :] = ids


def pair(student, teacher, ids, text, text_ids):
    rows, width = student.shape
    half_scale = 0.5 * SOFTMAX_TEMP_VALUE / float(width) ** 0.5
    contract = (((1,), (1,)), ((), ()))
    half_z = (
        lax.dot_general(student, text, contract, preferred_element_type=F32) * half_scale
        + 0.5 * LOGIT_BIAS
    )
    half_w = (
        lax.dot_general(teacher, text, contract, preferred_element_type=F32) * half_scale
        + 0.5 * LOGIT_BIAS
    )
    column = jnp.transpose(jnp.broadcast_to(ids, (LANES, rows)))
    column = jnp.concatenate([column] * (rows // LANES), axis=1)
    shift = jnp.where(column == text_ids, 0.75, 0.25)
    target = 0.25 * jnp.tanh(half_w) + shift
    tanh_z = jnp.tanh(half_z)
    slope = (0.5 * tanh_z + 0.5) - target
    z = half_z + half_z
    loss = (jnp.maximum(z, 0.0) - target * z) - jnp.log(0.5 * jnp.abs(tanh_z) + 0.5)
    folded = sum(loss[:, k : k + LANES] for k in range(0, rows, LANES))
    return slope.astype(BF16), folded


def text_term(slope, student):
    return lax.dot_general(slope, student, (((0,), (0,)), ((), ())), preferred_element_type=F32)


def unpacked(ref, rows):
    width = (ref.shape[0] - EXTRA) * LANES // rows
    return taken(ref, 0, rows, width), ids_of(ref, rows)


def both_images(ref, rows):
    size = (ref.shape[0] - EXTRA) // 2
    width = size * LANES // rows
    return taken(ref, 0, rows, width), taken(ref, size, rows, width), ids_of(ref, rows)


def block(images, texts):
    student, teacher, ids = images
    slope, folded = pair(student, teacher, ids, *texts)
    grad = jnp.dot(slope, texts[0], preferred_element_type=F32)
    return grad, folded, text_term(slope, student)


def add_to(sums_ref, sums_in, grad, folded):
    width = grad.shape[1]
    sums_ref[:, :width] = sums_in[:, :width] + grad
    sums_ref[:, width:] = sums_in[:, width:] + folded


def own_first(own_ref, text_ref, sums_ref, term_ref):
    rows, width = term_ref.shape
    images = both_images(own_ref, rows)
    sums_ref[:, :width], sums_ref[:, width:], term_ref[...] = block(images, unpacked(text_ref, rows))


def other_first(other_ref, text_ref, term_in, sums_ref, term_ref):
    rows, width = term_ref.shape
    images = both_images(other_ref, rows)
    sums_ref[:, :width], sums_ref[:, width:], term = block(images, unpacked(text_ref, rows))
    term_ref[...] = term_in[...] + term


def both_second(own_ref, other_ref, text_ref, own_in, other_in, own_out, other_out, term_ref):
    rows = term_ref.shape[0]
    text = unpacked(text_ref, rows)
    grad, folded, term = block(both_images(own_ref, rows), text)
    add_to(own_out, own_in, grad, folded)
    grad, folded, more = block(both_images(other_ref, rows), text)
    add_to(other_out, other_in, grad, folded)
    term_ref[...] = (term + more).astype(term_ref.dtype)


def both_near(
    own_ref, other_ref, text_ref, own_in, other_in, term_in, own_out, other_out, term_ref
):
    rows = term_ref.shape[0]
    text = unpacked(text_ref, rows)
    grad, folded, term = block(both_images(own_ref, rows), text)
    add_to(own_out, own_in, grad, folded)
    grad, folded, more = block(both_images(other_ref, rows), text)
    add_to(other_out, other_in, grad, folded)
    term_ref[...] = (term_in[...] + term + more).astype(term_ref.dtype)


def loss_row(folded):
    return jnp.sum(jnp.transpose(folded), axis=0, keepdims=True)


def ahead_near(student_ref, teacher_ref, near_ref, ahead_out, term_ref):
    rows = term_ref.shape[0]
    images = (student_ref[...], *unpacked(teacher_ref, rows))
    grad, folded, term_ref[...] = block(images, unpacked(near_ref, rows))
    put(ahead_out, 0, grad.astype(BF16))
    loss = loss_row(folded)
    high = loss.astype(BF16).astype(F32)
    ahead_out[ahead_out.shape[0] - EXTRA :, :] = spread(high, loss - high)


def gather_text(own_ref, second_ref, term_ref):
    term_ref[...] = own_ref[...] + second_ref[...].astype(F32)


def gather_images(own_ref, ahead_ref, sums_ref, loss_ref):
    rows, width = own_ref.shape[0], own_ref.shape[1] - LANES
    sums_ref[...] = own_ref[:, :width] + taken(ahead_ref, 0, rows, width).astype(F32)
    high, low = gathered(ahead_ref, ahead_ref.shape[0] - EXTRA, rows)
    loss_ref[...] = loss_row(own_ref[:, width:]) + high + low


def finish(sums_in, loss_in, term_in, other_ref, grad_ref, text_ref, loss_ref):
    rows, width = grad_ref.shape
    scale = SOFTMAX_TEMP_VALUE / float(width) ** 0.5
    text_ref[...] = term_in[...] * scale
    grad_ref[...] = (sums_in[...] + other_ref[:, :width]) * scale
    loss = loss_in[...] + loss_row(other_ref[:, width:])
    loss_ref[...] = (loss / float(WINDOW * rows)).reshape(rows)


def shards(student_image_vectors, teacher_emb, text_emb, species):
    rows, width = text_emb.shape
    dot = 2 * rows * rows * width

    def spec(n, m, dtype):
        return jax.ShapeDtypeStruct((n, m), dtype)

    sums = spec(rows, width + LANES, F32)
    term = spec(rows, width, F32)
    sent = spec(rows, width, BF16)
    packed = spec(rows * width // LANES + EXTRA, LANES, BF16)
    ahead_student = back(student_image_vectors)
    (text,) = call(pack_text, [packed], 0, text_emb, species)
    second = onward(text)
    near = across(text)
    images, teacher = call(
        pack_images,
        [spec(2 * rows * width // LANES + EXTRA, LANES, BF16), packed],
        0,
        student_image_vectors,
        teacher_emb,
        species,
        after=(text,),
    )
    other = within(images)
    ahead_teacher = back(teacher)
    own_sum, own_term = call(
        own_first, [sums, term], 64 * dot, images, text, after=(ahead_student,)
    )
    other_sum, own_term = call(other_first, [sums, term], 16 * dot, other, text, own_term)
    own_sum, other_sum, second_term = call(
        both_second, [sums, sums, sent], 16 * dot, images, other, second, own_sum, other_sum
    )
    second_back = back(second_term)
    ahead_sum, far_term = call(
        ahead_near,
        [packed, term],
        4 * dot,
        ahead_student,
        ahead_teacher,
        near,
        after=(second_term,),
    )
    ahead_back = onward(ahead_sum)
    own_sum, other_sum, near_term = call(
        both_near,
        [sums, sums, sent],
        0 * dot,
        images,
        other,
        near,
        own_sum,
        other_sum,
        far_term,
    )
    near_back = across(near_term)
    other_back = within(other_sum)
    (own_term,) = call(gather_text, [term], 128 * dot, own_term, second_back)
    own_sum, loss = call(
        gather_images, [term, spec(1, rows, F32)], 64 * dot, own_sum, ahead_back, after=(own_term,)
    )
    (own_term,) = call(
        gather_text, [term], 32 * dot, own_term, near_back, after=(own_sum,)
    )
    grad_student, grad_text, loss = call(
        finish,
        [term, term, jax.ShapeDtypeStruct((rows,), F32)],
        0,
        own_sum,
        loss,
        own_term,
        other_back,
    )
    return grad_student, grad_text, loss


def solution(mesh):
    return jax.shard_map(
        shards,
        mesh=mesh,
        in_specs=(P("dp", None), P("dp", None), P("dp", None), P("dp")),
        out_specs=(P("dp", None), P("dp", None), P("dp")),
        check_vma=False,
    )
```

```python
import jax
import jax.numpy as jnp
from jax import lax
from jax.experimental import pallas as pl
from jax.experimental.pallas import tpu as pltpu
from jax.sharding import PartitionSpec as P

SOFTMAX_TEMP_VALUE = 4.0
LOGIT_BIAS = -3.0
WINDOW = 7
DIGIT = 32.0
LANES = 128
EXTRA = 16

BF16 = jnp.bfloat16
F32 = jnp.float32


def moved(value, even, odd):
    length = lax.axis_size("dp")
    return lax.ppermute(
        value, "dp", [(i, (i + (odd if i % 2 else even)) % length) for i in range(length)]
    )


def within(value):
    return moved(value, 1, -1)


def across(value):
    return moved(value, -1, 1)


def onward(value):
    return moved(value, 2, -2)


def back(value):
    return moved(value, -2, 2)


def call(body, out_shape, flops, *args, after=()):
    count = len(args)

    def ordered(*refs):
        body(*refs[:count], *refs[count + len(after) :])

    in_bytes = sum(a.size * a.dtype.itemsize for a in args)
    out_bytes = sum(o.size * o.dtype.itemsize for o in out_shape)
    return pl.pallas_call(
        ordered,
        out_shape=out_shape,
        in_specs=[pl.BlockSpec(memory_space=pltpu.VMEM)] * count
        + [pl.BlockSpec(memory_space=pl.ANY)] * len(after),
        out_specs=[pl.BlockSpec(memory_space=pltpu.VMEM)] * len(out_shape),
        compiler_params=pltpu.CompilerParams(vmem_limit_bytes=40 * 1024 * 1024),
        cost_estimate=pl.CostEstimate(
            flops=flops, bytes_accessed=in_bytes + out_bytes, transcendentals=0
        ),
    )(*args, *after)


def spread(first, second):
    tiles = [
        row[:, k : k + LANES] for row in (first, second) for k in range(0, row.shape[1], LANES)
    ]
    place = lax.broadcasted_iota(jnp.int32, (EXTRA, LANES), 0)
    out = jnp.zeros((EXTRA, LANES), F32)
    for k, tile in enumerate(tiles):
        out = jnp.where(place == k, tile, out)
    return out.astype(BF16)


def gathered(ref, start, rows):
    tiles = ref[start:, :].astype(F32)
    count = rows // LANES
    first = jnp.concatenate([tiles[k : k + 1, :] for k in range(count)], axis=1)
    second = jnp.concatenate([tiles[k : k + 1, :] for k in range(count, 2 * count)], axis=1)
    return first, second


def digits(species):
    ids = species.reshape(1, species.shape[0]).astype(F32)
    high = jnp.floor(ids / DIGIT)
    return spread(high, ids - high * DIGIT)


def ids_of(ref, rows):
    high, low = gathered(ref, ref.shape[0] - EXTRA, rows)
    return high * DIGIT + low


def put(out_ref, start, value):
    rows = value.shape[0]
    for k in range(value.shape[1] // LANES):
        out_ref[start + k * rows : start + (k + 1) * rows, :] = value[:, k * LANES : (k + 1) * LANES]


def taken(ref, start, rows, width):
    count = width // LANES
    tiles = [ref[start + k * rows : start + (k + 1) * rows, :] for k in range(count)]
    return jnp.concatenate(tiles, axis=1)


def pack_text(text_ref, species_ref, out_ref):
    put(out_ref, 0, text_ref[...])
    out_ref[out_ref.shape[0] - EXTRA :, :] = digits(species_ref[...])


def pack_images(student_ref, teacher_ref, species_ref, out_ref, teacher_out):
    rows, width = student_ref.shape
    ids = digits(species_ref[...])
    put(out_ref, 0, student_ref[...])
    put(out_ref, rows * width // LANES, teacher_ref[...])
    out_ref[out_ref.shape[0] - EXTRA :, :] = ids
    put(teacher_out, 0, teacher_ref[...])
    teacher_out[teacher_out.shape[0] - EXTRA :, :] = ids


def pair(student, teacher, ids, text, text_ids):
    rows, width = student.shape
    half_scale = 0.5 * SOFTMAX_TEMP_VALUE / float(width) ** 0.5
    contract = (((1,), (1,)), ((), ()))
    half_z = (
        lax.dot_general(student, text, contract, preferred_element_type=F32) * half_scale
        + 0.5 * LOGIT_BIAS
    )
    half_w = (
        lax.dot_general(teacher, text, contract, preferred_element_type=F32) * half_scale
        + 0.5 * LOGIT_BIAS
    )
    column = jnp.transpose(jnp.broadcast_to(ids, (LANES, rows)))
    column = jnp.concatenate([column] * (rows // LANES), axis=1)
    shift = jnp.where(column == text_ids, 0.75, 0.25)
    target = 0.25 * jnp.tanh(half_w) + shift
    tanh_z = jnp.tanh(half_z)
    slope = (0.5 * tanh_z + 0.5) - target
    z = half_z + half_z
    loss = (jnp.maximum(z, 0.0) - target * z) - jnp.log(0.5 * jnp.abs(tanh_z) + 0.5)
    folded = sum(loss[:, k : k + LANES] for k in range(0, rows, LANES))
    return slope.astype(BF16), folded


def text_term(slope, student):
    return lax.dot_general(slope, student, (((0,), (0,)), ((), ())), preferred_element_type=F32)


def unpacked(ref, rows):
    width = (ref.shape[0] - EXTRA) * LANES // rows
    return taken(ref, 0, rows, width), ids_of(ref, rows)


def both_images(ref, rows):
    size = (ref.shape[0] - EXTRA) // 2
    width = size * LANES // rows
    return taken(ref, 0, rows, width), taken(ref, size, rows, width), ids_of(ref, rows)


def block(images, texts):
    student, teacher, ids = images
    slope, folded = pair(student, teacher, ids, *texts)
    grad = jnp.dot(slope, texts[0], preferred_element_type=F32)
    return grad, folded, text_term(slope, student)


def add_to(sums_ref, sums_in, grad, folded):
    width = grad.shape[1]
    sums_ref[:, :width] = sums_in[:, :width] + grad
    sums_ref[:, width:] = sums_in[:, width:] + folded


def own_first(own_ref, text_ref, sums_ref, term_ref):
    rows, width = term_ref.shape
    images = both_images(own_ref, rows)
    sums_ref[:, :width], sums_ref[:, width:], term_ref[...] = block(images, unpacked(text_ref, rows))


def other_first(other_ref, text_ref, term_in, sums_ref, term_ref):
    rows, width = term_ref.shape
    images = both_images(other_ref, rows)
    sums_ref[:, :width], sums_ref[:, width:], term = block(images, unpacked(text_ref, rows))
    term_ref[...] = term_in[...] + term


def both_second(own_ref, other_ref, text_ref, own_in, other_in, own_out, other_out, term_ref):
    rows = term_ref.shape[0]
    text = unpacked(text_ref, rows)
    grad, folded, term = block(both_images(own_ref, rows), text)
    add_to(own_out, own_in, grad, folded)
    grad, folded, more = block(both_images(other_ref, rows), text)
    add_to(other_out, other_in, grad, folded)
    term_ref[...] = (term + more).astype(term_ref.dtype)


def both_near(own_ref, other_ref, text_ref, own_in, other_in, own_out, other_out, term_ref):
    rows = term_ref.shape[0]
    text = unpacked(text_ref, rows)
    grad, folded, term = block(both_images(own_ref, rows), text)
    add_to(own_out, own_in, grad, folded)
    grad, folded, more = block(both_images(other_ref, rows), text)
    add_to(other_out, other_in, grad, folded)
    term_ref[...] = term + more


def loss_row(folded):
    return jnp.sum(jnp.transpose(folded), axis=0, keepdims=True)


def ahead_near(student_ref, teacher_ref, near_ref, term_in, ahead_out, term_ref):
    rows = term_ref.shape[0]
    images = (student_ref[...], *unpacked(teacher_ref, rows))
    grad, folded, term = block(images, unpacked(near_ref, rows))
    term_ref[...] = (term_in[...] + term).astype(term_ref.dtype)
    put(ahead_out, 0, grad.astype(BF16))
    loss = loss_row(folded)
    high = loss.astype(BF16).astype(F32)
    ahead_out[ahead_out.shape[0] - EXTRA :, :] = spread(high, loss - high)


def gather_text(own_ref, second_ref, term_ref):
    term_ref[...] = own_ref[...] + second_ref[...].astype(F32)


def gather_images(own_ref, ahead_ref, sums_ref, loss_ref):
    rows, width = own_ref.shape[0], own_ref.shape[1] - LANES
    sums_ref[...] = own_ref[:, :width] + taken(ahead_ref, 0, rows, width).astype(F32)
    high, low = gathered(ahead_ref, ahead_ref.shape[0] - EXTRA, rows)
    loss_ref[...] = loss_row(own_ref[:, width:]) + high + low


def finish(sums_in, loss_in, term_in, other_ref, grad_ref, text_ref, loss_ref):
    rows, width = grad_ref.shape
    scale = SOFTMAX_TEMP_VALUE / float(width) ** 0.5
    text_ref[...] = term_in[...] * scale
    grad_ref[...] = (sums_in[...] + other_ref[:, :width]) * scale
    loss = loss_in[...] + loss_row(other_ref[:, width:])
    loss_ref[...] = (loss / float(WINDOW * rows)).reshape(rows)


def shards(student_image_vectors, teacher_emb, text_emb, species):
    rows, width = text_emb.shape
    dot = 2 * rows * rows * width

    def spec(n, m, dtype):
        return jax.ShapeDtypeStruct((n, m), dtype)

    sums = spec(rows, width + LANES, F32)
    term = spec(rows, width, F32)
    sent = spec(rows, width, BF16)
    packed = spec(rows * width // LANES + EXTRA, LANES, BF16)
    ahead_student = back(student_image_vectors)
    (text,) = call(pack_text, [packed], 0, text_emb, species)
    second = onward(text)
    near = across(text)
    images, teacher = call(
        pack_images,
        [spec(2 * rows * width // LANES + EXTRA, LANES, BF16), packed],
        0,
        student_image_vectors,
        teacher_emb,
        species,
        after=(text,),
    )
    other = within(images)
    ahead_teacher = back(teacher)
    own_sum, own_term = call(
        own_first, [sums, term], 64 * dot, images, text, after=(ahead_student,)
    )
    other_sum, own_term = call(other_first, [sums, term], 16 * dot, other, text, own_term)
    own_sum, other_sum, second_term = call(
        both_second, [sums, sums, sent], 16 * dot, images, other, second, own_sum, other_sum
    )
    second_back = back(second_term)
    own_sum, other_sum, near_term = call(
        both_near, [sums, sums, term], 0 * dot, images, other, near, own_sum, other_sum
    )
    ahead_sum, near_term = call(
        ahead_near, [packed, sent], 0 * dot, ahead_student, ahead_teacher, near, near_term
    )
    ahead_back = onward(ahead_sum)
    near_back = across(near_term)
    other_back = within(other_sum)
    (own_term,) = call(gather_text, [term], 128 * dot, own_term, second_back)
    own_sum, loss = call(
        gather_images, [term, spec(1, rows, F32)], 64 * dot, own_sum, ahead_back, after=(own_term,)
    )
    (own_term,) = call(
        gather_text, [term], 32 * dot, own_term, near_back, after=(own_sum,)
    )
    grad_student, grad_text, loss = call(
        finish,
        [term, term, jax.ShapeDtypeStruct((rows,), F32)],
        0,
        own_sum,
        loss,
        own_term,
        other_back,
    )
    return grad_student, grad_text, loss


def solution(mesh):
    return jax.shard_map(
        shards,
        mesh=mesh,
        in_specs=(P("dp", None), P("dp", None), P("dp", None), P("dp")),
        out_specs=(P("dp", None), P("dp", None), P("dp")),
        check_vma=False,
    )
```

```python
import jax
import jax.numpy as jnp
from jax import lax
from jax.experimental import pallas as pl
from jax.experimental.pallas import tpu as pltpu
from jax.sharding import PartitionSpec as P

SOFTMAX_TEMP_VALUE = 4.0
LOGIT_BIAS = -3.0
WINDOW = 7
DIGIT = 32.0
LANES = 128
EXTRA = 16

BF16 = jnp.bfloat16
F32 = jnp.float32


def moved(value, even, odd):
    length = lax.axis_size("dp")
    return lax.ppermute(
        value, "dp", [(i, (i + (odd if i % 2 else even)) % length) for i in range(length)]
    )


def within(value):
    return moved(value, 1, -1)


def across(value):
    return moved(value, -1, 1)


def onward(value):
    return moved(value, 2, -2)


def back(value):
    return moved(value, -2, 2)


def call(body, out_shape, flops, *args, after=()):
    count = len(args)

    def ordered(*refs):
        body(*refs[:count], *refs[count + len(after) :])

    in_bytes = sum(a.size * a.dtype.itemsize for a in args)
    out_bytes = sum(o.size * o.dtype.itemsize for o in out_shape)
    return pl.pallas_call(
        ordered,
        out_shape=out_shape,
        in_specs=[pl.BlockSpec(memory_space=pltpu.VMEM)] * count
        + [pl.BlockSpec(memory_space=pl.ANY)] * len(after),
        out_specs=[pl.BlockSpec(memory_space=pltpu.VMEM)] * len(out_shape),
        compiler_params=pltpu.CompilerParams(vmem_limit_bytes=40 * 1024 * 1024),
        cost_estimate=pl.CostEstimate(
            flops=flops, bytes_accessed=in_bytes + out_bytes, transcendentals=0
        ),
    )(*args, *after)


def spread(first, second):
    tiles = [
        row[:, k : k + LANES] for row in (first, second) for k in range(0, row.shape[1], LANES)
    ]
    place = lax.broadcasted_iota(jnp.int32, (EXTRA, LANES), 0)
    out = jnp.zeros((EXTRA, LANES), F32)
    for k, tile in enumerate(tiles):
        out = jnp.where(place == k, tile, out)
    return out.astype(BF16)


def gathered(ref, start, rows):
    tiles = ref[start:, :].astype(F32)
    count = rows // LANES
    first = jnp.concatenate([tiles[k : k + 1, :] for k in range(count)], axis=1)
    second = jnp.concatenate([tiles[k : k + 1, :] for k in range(count, 2 * count)], axis=1)
    return first, second


def digits(species):
    ids = species.reshape(1, species.shape[0]).astype(F32)
    high = jnp.floor(ids / DIGIT)
    return spread(high, ids - high * DIGIT)


def ids_of(ref, rows):
    high, low = gathered(ref, ref.shape[0] - EXTRA, rows)
    return high * DIGIT + low


def put(out_ref, start, value):
    rows = value.shape[0]
    for k in range(value.shape[1] // LANES):
        out_ref[start + k * rows : start + (k + 1) * rows, :] = value[:, k * LANES : (k + 1) * LANES]


def taken(ref, start, rows, width):
    count = width // LANES
    tiles = [ref[start + k * rows : start + (k + 1) * rows, :] for k in range(count)]
    return jnp.concatenate(tiles, axis=1)


def write_ids(species_ref, ids_ref):
    ids_ref[...] = digits(species_ref[...])


def pack_text(text_ref, ids_ref, out_ref):
    put(out_ref, 0, text_ref[...])
    out_ref[out_ref.shape[0] - EXTRA :, :] = ids_ref[...]


def pack_images(student_ref, teacher_ref, ids_ref, out_ref, teacher_out):
    rows, width = student_ref.shape
    put(out_ref, 0, student_ref[...])
    put(out_ref, rows * width // LANES, teacher_ref[...])
    out_ref[out_ref.shape[0] - EXTRA :, :] = ids_ref[...]
    put(teacher_out, 0, teacher_ref[...])
    teacher_out[teacher_out.shape[0] - EXTRA :, :] = ids_ref[...]


def pair(student, teacher, ids, text, text_ids):
    rows, width = student.shape
    half_scale = 0.5 * SOFTMAX_TEMP_VALUE / float(width) ** 0.5
    contract = (((1,), (1,)), ((), ()))
    half_z = (
        lax.dot_general(student, text, contract, preferred_element_type=F32) * half_scale
        + 0.5 * LOGIT_BIAS
    )
    half_w = (
        lax.dot_general(teacher, text, contract, preferred_element_type=F32) * half_scale
        + 0.5 * LOGIT_BIAS
    )
    column = jnp.transpose(jnp.broadcast_to(ids, (LANES, rows)))
    column = jnp.concatenate([column] * (rows // LANES), axis=1)
    shift = jnp.where(column == text_ids, 0.75, 0.25)
    target = 0.25 * jnp.tanh(half_w) + shift
    tanh_z = jnp.tanh(half_z)
    slope = (0.5 * tanh_z + 0.5) - target
    z = half_z + half_z
    loss = (jnp.maximum(z, 0.0) - target * z) - jnp.log(0.5 * jnp.abs(tanh_z) + 0.5)
    folded = sum(loss[:, k : k + LANES] for k in range(0, rows, LANES))
    return slope.astype(BF16), folded


def text_term(slope, student):
    return lax.dot_general(slope, student, (((0,), (0,)), ((), ())), preferred_element_type=F32)


def unpacked(ref, rows):
    width = (ref.shape[0] - EXTRA) * LANES // rows
    return taken(ref, 0, rows, width), ids_of(ref, rows)


def both_images(ref, rows):
    size = (ref.shape[0] - EXTRA) // 2
    width = size * LANES // rows
    return taken(ref, 0, rows, width), taken(ref, size, rows, width), ids_of(ref, rows)


def block(images, texts):
    student, teacher, ids = images
    slope, folded = pair(student, teacher, ids, *texts)
    grad = jnp.dot(slope, texts[0], preferred_element_type=F32)
    return grad, folded, text_term(slope, student)


def two_blocks(images, texts, sums_in, sums_out):
    rows, width = texts[0].shape
    pairs = [pair(student, teacher, ids, *texts) for student, teacher, ids in images]
    slope = jnp.concatenate([slope for slope, _ in pairs], axis=0)
    grad = jnp.dot(slope, texts[0], preferred_element_type=F32)
    for k, (was, out) in enumerate(zip(sums_in, sums_out)):
        out[:, :width] = was[:, :width] + grad[k * rows : (k + 1) * rows, :]
        out[:, width:] = was[:, width:] + pairs[k][1]
    return text_term(slope, jnp.concatenate([student for student, _, _ in images], axis=0))


def own_first(own_ref, text_ref, sums_ref, term_ref):
    rows, width = term_ref.shape
    images = both_images(own_ref, rows)
    sums_ref[:, :width], sums_ref[:, width:], term_ref[...] = block(images, unpacked(text_ref, rows))


def other_first(other_ref, text_ref, term_in, sums_ref, term_ref):
    rows, width = term_ref.shape
    images = both_images(other_ref, rows)
    sums_ref[:, :width], sums_ref[:, width:], term = block(images, unpacked(text_ref, rows))
    term_ref[...] = term_in[...] + term


def both_second(
    own_ref, other_ref, text_ref, ids_ref, own_in, other_in, own_out, other_out, term_ref
):
    rows = term_ref.shape[0]
    images = [both_images(ref, rows) for ref in (own_ref, other_ref)]
    sums_in, sums_out = (own_in, other_in), (own_out, other_out)
    texts = (text_ref[...], ids_of(ids_ref, rows))
    term = two_blocks(images, texts, sums_in, sums_out)
    term_ref[...] = term.astype(term_ref.dtype)


def both_near(
    own_ref, other_ref, text_ref, own_in, other_in, term_in, own_out, other_out, term_ref
):
    rows = term_ref.shape[0]
    images = [both_images(ref, rows) for ref in (own_ref, other_ref)]
    sums_in, sums_out = (own_in, other_in), (own_out, other_out)
    term = two_blocks(images, unpacked(text_ref, rows), sums_in, sums_out)
    term_ref[...] = (term_in[...] + term).astype(term_ref.dtype)


def loss_row(folded):
    return jnp.sum(jnp.transpose(folded), axis=0, keepdims=True)


def ahead_near(student_ref, teacher_ref, near_ref, ahead_out, term_ref):
    rows = term_ref.shape[0]
    images = (student_ref[...], *unpacked(teacher_ref, rows))
    grad, folded, term_ref[...] = block(images, unpacked(near_ref, rows))
    put(ahead_out, 0, grad.astype(BF16))
    loss = loss_row(folded)
    high = loss.astype(BF16).astype(F32)
    ahead_out[ahead_out.shape[0] - EXTRA :, :] = spread(high, loss - high)


def gather_text(own_ref, second_ref, term_ref):
    term_ref[...] = own_ref[...] + second_ref[...].astype(F32)


def gather_images(own_ref, ahead_ref, sums_ref, loss_ref):
    rows, width = own_ref.shape[0], own_ref.shape[1] - LANES
    sums_ref[...] = own_ref[:, :width] + taken(ahead_ref, 0, rows, width).astype(F32)
    high, low = gathered(ahead_ref, ahead_ref.shape[0] - EXTRA, rows)
    loss_ref[...] = loss_row(own_ref[:, width:]) + high + low


def finish(sums_in, loss_in, term_in, other_ref, grad_ref, text_ref, loss_ref):
    rows, width = grad_ref.shape
    scale = SOFTMAX_TEMP_VALUE / float(width) ** 0.5
    text_ref[...] = term_in[...] * scale
    grad_ref[...] = (sums_in[...] + other_ref[:, :width]) * scale
    loss = loss_in[...] + loss_row(other_ref[:, width:])
    loss_ref[...] = (loss / float(WINDOW * rows)).reshape(rows)


def shards(student_image_vectors, teacher_emb, text_emb, species):
    rows, width = text_emb.shape
    dot = 2 * rows * rows * width

    def spec(n, m, dtype):
        return jax.ShapeDtypeStruct((n, m), dtype)

    sums = spec(rows, width + LANES, F32)
    term = spec(rows, width, F32)
    sent = spec(rows, width, BF16)
    packed = spec(rows * width // LANES + EXTRA, LANES, BF16)
    ahead_student = back(student_image_vectors)
    second = onward(text_emb)
    (ids,) = call(write_ids, [spec(EXTRA, LANES, BF16)], 0, species)
    second_ids = onward(ids)
    (text,) = call(pack_text, [packed], 0, text_emb, ids)
    near = across(text)
    images, teacher = call(
        pack_images,
        [spec(2 * rows * width // LANES + EXTRA, LANES, BF16), packed],
        0,
        student_image_vectors,
        teacher_emb,
        ids,
        after=(text,),
    )
    other = within(images)
    ahead_teacher = back(teacher)
    own_sum, own_term = call(
        own_first, [sums, term], 64 * dot, images, text, after=(ahead_student,)
    )
    other_sum, own_term = call(other_first, [sums, term], 16 * dot, other, text, own_term)
    own_sum, other_sum, second_term = call(
        both_second, [sums, sums, sent], 16 * dot, images, other, second, second_ids, own_sum, other_sum
    )
    second_back = back(second_term)
    ahead_sum, far_term = call(
        ahead_near,
        [packed, term],
        4 * dot,
        ahead_student,
        ahead_teacher,
        near,
        after=(second_term,),
    )
    ahead_back = onward(ahead_sum)
    own_sum, other_sum, near_term = call(
        both_near,
        [sums, sums, sent],
        0 * dot,
        images,
        other,
        near,
        own_sum,
        other_sum,
        far_term,
    )
    near_back = across(near_term)
    other_back = within(other_sum)
    (own_term,) = call(gather_text, [term], 128 * dot, own_term, second_back)
    own_sum, loss = call(
        gather_images, [term, spec(1, rows, F32)], 64 * dot, own_sum, ahead_back, after=(own_term,)
    )
    (own_term,) = call(
        gather_text, [term], 32 * dot, own_term, near_back, after=(own_sum,)
    )
    grad_student, grad_text, loss = call(
        finish,
        [term, term, jax.ShapeDtypeStruct((rows,), F32)],
        0,
        own_sum,
        loss,
        own_term,
        other_back,
    )
    return grad_student, grad_text, loss


def solution(mesh):
    return jax.shard_map(
        shards,
        mesh=mesh,
        in_specs=(P("dp", None), P("dp", None), P("dp", None), P("dp")),
        out_specs=(P("dp", None), P("dp", None), P("dp")),
        check_vma=False,
    )
```

```python
import jax
import jax.numpy as jnp
from jax import lax
from jax.experimental import pallas as pl
from jax.experimental.pallas import tpu as pltpu
from jax.sharding import PartitionSpec as P

SOFTMAX_TEMP_VALUE = 4.0
LOGIT_BIAS = -3.0
WINDOW = 7
DIGIT = 32.0
LANES = 128
EXTRA = 16

BF16 = jnp.bfloat16
F32 = jnp.float32


def moved(value, even, odd):
    length = lax.axis_size("dp")
    return lax.ppermute(
        value, "dp", [(i, (i + (odd if i % 2 else even)) % length) for i in range(length)]
    )


def within(value):
    return moved(value, 1, -1)


def across(value):
    return moved(value, -1, 1)


def onward(value):
    return moved(value, 2, -2)


def back(value):
    return moved(value, -2, 2)


def far_back(value):
    return moved(value, -3, 3)


def call(body, out_shape, flops, *args, after=()):
    count = len(args)

    def ordered(*refs):
        body(*refs[:count], *refs[count + len(after) :])

    in_bytes = sum(a.size * a.dtype.itemsize for a in args)
    out_bytes = sum(o.size * o.dtype.itemsize for o in out_shape)
    return pl.pallas_call(
        ordered,
        out_shape=out_shape,
        in_specs=[pl.BlockSpec(memory_space=pltpu.VMEM)] * count
        + [pl.BlockSpec(memory_space=pl.ANY)] * len(after),
        out_specs=[pl.BlockSpec(memory_space=pltpu.VMEM)] * len(out_shape),
        compiler_params=pltpu.CompilerParams(vmem_limit_bytes=40 * 1024 * 1024),
        cost_estimate=pl.CostEstimate(
            flops=flops, bytes_accessed=in_bytes + out_bytes, transcendentals=0
        ),
    )(*args, *after)


def spread(first, second):
    tiles = [
        row[:, k : k + LANES] for row in (first, second) for k in range(0, row.shape[1], LANES)
    ]
    place = lax.broadcasted_iota(jnp.int32, (EXTRA, LANES), 0)
    out = jnp.zeros((EXTRA, LANES), F32)
    for k, tile in enumerate(tiles):
        out = jnp.where(place == k, tile, out)
    return out.astype(BF16)


def gathered(ref, start, rows):
    tiles = ref[start:, :].astype(F32)
    count = rows // LANES
    first = jnp.concatenate([tiles[k : k + 1, :] for k in range(count)], axis=1)
    second = jnp.concatenate([tiles[k : k + 1, :] for k in range(count, 2 * count)], axis=1)
    return first, second


def digits(species):
    ids = species.reshape(1, species.shape[0]).astype(F32)
    high = jnp.floor(ids / DIGIT)
    return spread(high, ids - high * DIGIT)


def ids_of(ref, rows):
    high, low = gathered(ref, ref.shape[0] - EXTRA, rows)
    return high * DIGIT + low


def put(out_ref, start, value):
    rows = value.shape[0]
    for k in range(value.shape[1] // LANES):
        out_ref[start + k * rows : start + (k + 1) * rows, :] = value[:, k * LANES : (k + 1) * LANES]


def taken(ref, start, rows, width):
    count = width // LANES
    tiles = [ref[start + k * rows : start + (k + 1) * rows, :] for k in range(count)]
    return jnp.concatenate(tiles, axis=1)


def pack_text(text_ref, species_ref, out_ref):
    put(out_ref, 0, text_ref[...])
    out_ref[out_ref.shape[0] - EXTRA :, :] = digits(species_ref[...])


def pack_images(student_ref, teacher_ref, species_ref, out_ref):
    rows, width = student_ref.shape
    put(out_ref, 0, student_ref[...])
    put(out_ref, rows * width // LANES, teacher_ref[...])
    out_ref[out_ref.shape[0] - EXTRA :, :] = digits(species_ref[...])


def pair(student, teacher, ids, text, text_ids):
    rows, width = student.shape
    half_scale = 0.5 * SOFTMAX_TEMP_VALUE / float(width) ** 0.5
    contract = (((1,), (1,)), ((), ()))
    half_z = (
        lax.dot_general(student, text, contract, preferred_element_type=F32) * half_scale
        + 0.5 * LOGIT_BIAS
    )
    half_w = (
        lax.dot_general(teacher, text, contract, preferred_element_type=F32) * half_scale
        + 0.5 * LOGIT_BIAS
    )
    column = jnp.transpose(jnp.broadcast_to(ids, (LANES, rows)))
    column = jnp.concatenate([column] * (rows // LANES), axis=1)
    shift = jnp.where(column == text_ids, 0.75, 0.25)
    target = 0.25 * jnp.tanh(half_w) + shift
    tanh_z = jnp.tanh(half_z)
    slope = (0.5 * tanh_z + 0.5) - target
    z = half_z + half_z
    loss = (jnp.maximum(z, 0.0) - target * z) - jnp.log(0.5 * jnp.abs(tanh_z) + 0.5)
    folded = sum(loss[:, k : k + LANES] for k in range(0, rows, LANES))
    return slope.astype(BF16), folded


def text_term(slope, student):
    return lax.dot_general(slope, student, (((0,), (0,)), ((), ())), preferred_element_type=F32)


def unpacked(ref, rows):
    width = (ref.shape[0] - EXTRA) * LANES // rows
    return taken(ref, 0, rows, width), ids_of(ref, rows)


def both_images(ref, rows):
    size = (ref.shape[0] - EXTRA) // 2
    width = size * LANES // rows
    return taken(ref, 0, rows, width), taken(ref, size, rows, width), ids_of(ref, rows)


def block(images, texts):
    student, teacher, ids = images
    slope, folded = pair(student, teacher, ids, *texts)
    grad = jnp.dot(slope, texts[0], preferred_element_type=F32)
    return grad, folded, text_term(slope, student)


def two_blocks(images, texts, sums_in, sums_out):
    rows, width = texts[0].shape
    pairs = [pair(student, teacher, ids, *texts) for student, teacher, ids in images]
    slope = jnp.concatenate([slope for slope, _ in pairs], axis=0)
    grad = jnp.dot(slope, texts[0], preferred_element_type=F32)
    for k, (was, out) in enumerate(zip(sums_in, sums_out)):
        out[:, :width] = was[:, :width] + grad[k * rows : (k + 1) * rows, :]
        out[:, width:] = was[:, width:] + pairs[k][1]
    return text_term(slope, jnp.concatenate([student for student, _, _ in images], axis=0))


def own_first(own_ref, text_ref, sums_ref, term_ref):
    rows, width = term_ref.shape
    images = both_images(own_ref, rows)
    sums_ref[:, :width], sums_ref[:, width:], term_ref[...] = block(images, unpacked(text_ref, rows))


def add_to(sums_ref, sums_in, grad, folded):
    width = grad.shape[1]
    sums_ref[:, :width] = sums_in[:, :width] + grad
    sums_ref[:, width:] = sums_in[:, width:] + folded


def own_next(own_ref, text_ref, sums_in, sums_ref, term_ref):
    rows = term_ref.shape[0]
    grad, folded, term = block(both_images(own_ref, rows), unpacked(text_ref, rows))
    add_to(sums_ref, sums_in, grad, folded)
    term_ref[...] = term.astype(term_ref.dtype)


def other_two(
    other_ref, text_ref, near_ref, own_in, near_in, sums_ref, near_out, own_out
):
    rows, width = own_in.shape
    other = both_images(other_ref, rows)
    grad, folded, term = block(other, unpacked(near_ref, rows))
    near_out[...] = (near_in[...] + term).astype(near_out.dtype)
    sums_ref[:, :width] = grad
    sums_ref[:, width:] = folded
    grad, folded, term = block(other, unpacked(text_ref, rows))
    own_out[...] = own_in[...] + term
    add_to(sums_ref, sums_ref, grad, folded)


def both(own_ref, other_ref, text_ref, own_in, other_in, own_out, other_out, term_ref):
    rows = term_ref.shape[0]
    images = [both_images(ref, rows) for ref in (own_ref, other_ref)]
    sums_in, sums_out = (own_in, other_in), (own_out, other_out)
    term = two_blocks(images, unpacked(text_ref, rows), sums_in, sums_out)
    term_ref[...] = term.astype(term_ref.dtype)


def loss_row(folded):
    return jnp.sum(jnp.transpose(folded), axis=0, keepdims=True)


def gather(own_ref, back_ref, term_ref):
    term_ref[...] = own_ref[...] + back_ref[...].astype(F32)


def finish(own_ref, other_ref, term_in, grad_ref, text_ref, loss_ref):
    rows, width = grad_ref.shape
    scale = SOFTMAX_TEMP_VALUE / float(width) ** 0.5
    text_ref[...] = term_in[...] * scale
    grad_ref[...] = (own_ref[:, :width] + other_ref[:, :width]) * scale
    loss = loss_row(own_ref[:, width:] + other_ref[:, width:])
    loss_ref[...] = (loss / float(WINDOW * rows)).reshape(rows)


def shards(student_image_vectors, teacher_emb, text_emb, species):
    rows, width = text_emb.shape
    dot = 2 * rows * rows * width

    def spec(n, m, dtype):
        return jax.ShapeDtypeStruct((n, m), dtype)

    sums = spec(rows, width + LANES, F32)
    term = spec(rows, width, F32)
    sent = spec(rows, width, BF16)
    packed = spec(rows * width // LANES + EXTRA, LANES, BF16)
    (text,) = call(pack_text, [packed], 0, text_emb, species)
    near = across(text)
    second = onward(text)
    (images,) = call(
        pack_images,
        [spec(2 * rows * width // LANES + EXTRA, LANES, BF16)],
        0,
        student_image_vectors,
        teacher_emb,
        species,
        after=(text,),
    )
    other = within(images)
    far = onward(near)
    own_sum, own_term = call(own_first, [sums, term], 16 * dot, images, text)
    own_sum, near_term = call(own_next, [sums, term], 32 * dot, images, near, own_sum)
    other_sum, near_term, own_term = call(
        other_two, [sums, sent, term], 0 * dot, other, text, near, own_term, near_term
    )
    near_back = across(near_term)
    own_sum, other_sum, second_term = call(
        both, [sums, sums, sent], 0 * dot, images, other, second, own_sum, other_sum
    )
    second_back = back(second_term)
    own_sum, far_term = call(own_next, [sums, sent], 0 * dot, images, far, own_sum)
    last_back = far_back(far_term)
    other_back = within(other_sum)
    for value, weight in ((near_back, 64 * dot), (second_back, 64 * dot), (last_back, 32 * dot)):
        (own_term,) = call(gather, [term], weight, own_term, value)
    grad_student, grad_text, loss = call(
        finish,
        [term, term, jax.ShapeDtypeStruct((rows,), F32)],
        0,
        own_sum,
        other_back,
        own_term,
    )
    return grad_student, grad_text, loss


def solution(mesh):
    return jax.shard_map(
        shards,
        mesh=mesh,
        in_specs=(P("dp", None), P("dp", None), P("dp", None), P("dp")),
        out_specs=(P("dp", None), P("dp", None), P("dp")),
        check_vma=False,
    )
```

```python
import jax
import jax.numpy as jnp
from jax import lax
from jax.experimental import pallas as pl
from jax.experimental.pallas import tpu as pltpu
from jax.sharding import PartitionSpec as P

SOFTMAX_TEMP_VALUE = 4.0
LOGIT_BIAS = -3.0
WINDOW = 7
DIGIT = 32.0
LANES = 128
EXTRA = 16

BF16 = jnp.bfloat16
F32 = jnp.float32


def moved(value, even, odd):
    length = lax.axis_size("dp")
    return lax.ppermute(
        value, "dp", [(i, (i + (odd if i % 2 else even)) % length) for i in range(length)]
    )


def within(value):
    return moved(value, 1, -1)


def across(value):
    return moved(value, -1, 1)


def onward(value):
    return moved(value, 2, -2)


def back(value):
    return moved(value, -2, 2)


def call(body, out_shape, flops, *args, after=()):
    count = len(args)

    def ordered(*refs):
        body(*refs[:count], *refs[count + len(after) :])

    in_bytes = sum(a.size * a.dtype.itemsize for a in args)
    out_bytes = sum(o.size * o.dtype.itemsize for o in out_shape)
    return pl.pallas_call(
        ordered,
        out_shape=out_shape,
        in_specs=[pl.BlockSpec(memory_space=pltpu.VMEM)] * count
        + [pl.BlockSpec(memory_space=pl.ANY)] * len(after),
        out_specs=[pl.BlockSpec(memory_space=pltpu.VMEM)] * len(out_shape),
        compiler_params=pltpu.CompilerParams(vmem_limit_bytes=40 * 1024 * 1024),
        cost_estimate=pl.CostEstimate(
            flops=flops, bytes_accessed=in_bytes + out_bytes, transcendentals=0
        ),
    )(*args, *after)


def spread(first, second):
    tiles = [
        row[:, k : k + LANES] for row in (first, second) for k in range(0, row.shape[1], LANES)
    ]
    place = lax.broadcasted_iota(jnp.int32, (EXTRA, LANES), 0)
    out = jnp.zeros((EXTRA, LANES), F32)
    for k, tile in enumerate(tiles):
        out = jnp.where(place == k, tile, out)
    return out.astype(BF16)


def gathered(ref, start, rows):
    tiles = ref[start:, :].astype(F32)
    count = rows // LANES
    first = jnp.concatenate([tiles[k : k + 1, :] for k in range(count)], axis=1)
    second = jnp.concatenate([tiles[k : k + 1, :] for k in range(count, 2 * count)], axis=1)
    return first, second


def digits(species):
    ids = species.reshape(1, species.shape[0]).astype(F32)
    high = jnp.floor(ids / DIGIT)
    return spread(high, ids - high * DIGIT)


def ids_of(ref, rows):
    high, low = gathered(ref, ref.shape[0] - EXTRA, rows)
    return high * DIGIT + low


def put(out_ref, start, value):
    rows = value.shape[0]
    for k in range(value.shape[1] // LANES):
        out_ref[start + k * rows : start + (k + 1) * rows, :] = value[:, k * LANES : (k + 1) * LANES]


def taken(ref, start, rows, width):
    count = width // LANES
    tiles = [ref[start + k * rows : start + (k + 1) * rows, :] for k in range(count)]
    return jnp.concatenate(tiles, axis=1)


def pack_text(text_ref, species_ref, out_ref):
    put(out_ref, 0, text_ref[...])
    out_ref[out_ref.shape[0] - EXTRA :, :] = digits(species_ref[...])


def pack_images(student_ref, teacher_ref, species_ref, out_ref, teacher_out):
    rows, width = student_ref.shape
    ids = digits(species_ref[...])
    put(out_ref, 0, student_ref[...])
    put(out_ref, rows * width // LANES, teacher_ref[...])
    out_ref[out_ref.shape[0] - EXTRA :, :] = ids
    put(teacher_out, 0, teacher_ref[...])
    teacher_out[teacher_out.shape[0] - EXTRA :, :] = ids


def pair(student, teacher, ids, text, text_ids):
    rows, width = student.shape
    half_scale = 0.5 * SOFTMAX_TEMP_VALUE / float(width) ** 0.5
    contract = (((1,), (1,)), ((), ()))
    half_z = (
        lax.dot_general(student, text, contract, preferred_element_type=F32) * half_scale
        + 0.5 * LOGIT_BIAS
    )
    half_w = (
        lax.dot_general(teacher, text, contract, preferred_element_type=F32) * half_scale
        + 0.5 * LOGIT_BIAS
    )
    column = jnp.transpose(jnp.broadcast_to(ids, (LANES, rows)))
    column = jnp.concatenate([column] * (rows // LANES), axis=1)
    shift = jnp.where(column == text_ids, 0.75, 0.25)
    target = 0.25 * jnp.tanh(half_w) + shift
    tanh_z = jnp.tanh(half_z)
    slope = (0.5 * tanh_z + 0.5) - target
    z = half_z + half_z
    loss = (jnp.maximum(z, 0.0) - target * z) - jnp.log(0.5 * jnp.abs(tanh_z) + 0.5)
    folded = sum(loss[:, k : k + LANES] for k in range(0, rows, LANES))
    return slope.astype(BF16), folded


def text_term(slope, student):
    return lax.dot_general(slope, student, (((0,), (0,)), ((), ())), preferred_element_type=F32)


def unpacked(ref, rows):
    width = (ref.shape[0] - EXTRA) * LANES // rows
    return taken(ref, 0, rows, width), ids_of(ref, rows)


def both_images(ref, rows):
    size = (ref.shape[0] - EXTRA) // 2
    width = size * LANES // rows
    return taken(ref, 0, rows, width), taken(ref, size, rows, width), ids_of(ref, rows)


def block(images, texts):
    student, teacher, ids = images
    slope, folded = pair(student, teacher, ids, *texts)
    grad = jnp.dot(slope, texts[0], preferred_element_type=F32)
    return grad, folded, text_term(slope, student)


def two_blocks(images, texts, sums_in, sums_out):
    rows, width = texts[0].shape
    pairs = [pair(student, teacher, ids, *texts) for student, teacher, ids in images]
    slope = jnp.concatenate([slope for slope, _ in pairs], axis=0)
    grad = jnp.dot(slope, texts[0], preferred_element_type=F32)
    for k, (was, out) in enumerate(zip(sums_in, sums_out)):
        out[:, :width] = was[:, :width] + grad[k * rows : (k + 1) * rows, :]
        out[:, width:] = was[:, width:] + pairs[k][1]
    return text_term(slope, jnp.concatenate([student for student, _, _ in images], axis=0))


def own_first(own_ref, text_ref, sums_ref, term_ref, text_out):
    text_out[...] = text_ref[...]
    rows, width = term_ref.shape
    images = both_images(own_ref, rows)
    sums_ref[:, :width], sums_ref[:, width:], term_ref[...] = block(images, unpacked(text_ref, rows))


def other_first(other_ref, text_ref, term_in, sums_ref, term_ref):
    rows, width = term_ref.shape
    images = both_images(other_ref, rows)
    sums_ref[:, :width], sums_ref[:, width:], term = block(images, unpacked(text_ref, rows))
    term_ref[...] = term_in[...] + term


def both(own_ref, other_ref, text_ref, own_in, other_in, own_out, other_out, term_ref):
    rows = term_ref.shape[0]
    images = [both_images(ref, rows) for ref in (own_ref, other_ref)]
    sums_in, sums_out = (own_in, other_in), (own_out, other_out)
    term = two_blocks(images, unpacked(text_ref, rows), sums_in, sums_out)
    term_ref[...] = term.astype(term_ref.dtype)


def both_near(
    own_ref, other_ref, text_ref, own_in, other_in, term_in, own_out, other_out, term_ref
):
    rows = term_ref.shape[0]
    images = [both_images(ref, rows) for ref in (own_ref, other_ref)]
    sums_in, sums_out = (own_in, other_in), (own_out, other_out)
    term = two_blocks(images, unpacked(text_ref, rows), sums_in, sums_out)
    term_ref[...] = (term_in[...] + term).astype(term_ref.dtype)


def loss_row(folded):
    return jnp.sum(jnp.transpose(folded), axis=0, keepdims=True)


def ahead_near(student_ref, teacher_ref, near_ref, ahead_out, term_ref):
    rows = term_ref.shape[0]
    images = (student_ref[...], *unpacked(teacher_ref, rows))
    grad, folded, term_ref[...] = block(images, unpacked(near_ref, rows))
    put(ahead_out, 0, grad.astype(BF16))
    loss = loss_row(folded)
    high = loss.astype(BF16).astype(F32)
    ahead_out[ahead_out.shape[0] - EXTRA :, :] = spread(high, loss - high)


def gather_text(own_ref, second_ref, term_ref):
    term_ref[...] = own_ref[...] + second_ref[...].astype(F32)


def gather_images(own_ref, ahead_ref, sums_ref, loss_ref):
    rows, width = own_ref.shape[0], own_ref.shape[1] - LANES
    sums_ref[...] = own_ref[:, :width] + taken(ahead_ref, 0, rows, width).astype(F32)
    high, low = gathered(ahead_ref, ahead_ref.shape[0] - EXTRA, rows)
    loss_ref[...] = loss_row(own_ref[:, width:]) + high + low


def finish(sums_in, loss_in, term_in, other_ref, grad_ref, text_ref, loss_ref):
    rows, width = grad_ref.shape
    scale = SOFTMAX_TEMP_VALUE / float(width) ** 0.5
    text_ref[...] = term_in[...] * scale
    grad_ref[...] = (sums_in[...] + other_ref[:, :width]) * scale
    loss = loss_in[...] + loss_row(other_ref[:, width:])
    loss_ref[...] = (loss / float(WINDOW * rows)).reshape(rows)


def shards(student_image_vectors, teacher_emb, text_emb, species):
    rows, width = text_emb.shape
    dot = 2 * rows * rows * width

    def spec(n, m, dtype):
        return jax.ShapeDtypeStruct((n, m), dtype)

    sums = spec(rows, width + LANES, F32)
    term = spec(rows, width, F32)
    sent = spec(rows, width, BF16)
    packed = spec(rows * width // LANES + EXTRA, LANES, BF16)
    ahead_student = back(student_image_vectors)
    (text,) = call(pack_text, [packed], 0, text_emb, species)
    second = onward(text)
    images, teacher = call(
        pack_images,
        [spec(2 * rows * width // LANES + EXTRA, LANES, BF16), packed],
        0,
        student_image_vectors,
        teacher_emb,
        species,
        after=(text,),
    )
    other = within(images)
    ahead_teacher = back(teacher)
    own_sum, own_term, text_again = call(
        own_first,
        [sums, term, packed],
        64 * dot,
        images,
        text,
        after=(ahead_student,),
    )
    near = across(text_again)
    other_sum, own_term = call(other_first, [sums, term], 16 * dot, other, text, own_term)
    own_sum, other_sum, second_term = call(
        both, [sums, sums, sent], 16 * dot, images, other, second, own_sum, other_sum
    )
    second_back = back(second_term)
    ahead_sum, far_term = call(
        ahead_near,
        [packed, term],
        4 * dot,
        ahead_student,
        ahead_teacher,
        near,
        after=(second_term,),
    )
    ahead_back = onward(ahead_sum)
    own_sum, other_sum, near_term = call(
        both_near,
        [sums, sums, sent],
        0 * dot,
        images,
        other,
        near,
        own_sum,
        other_sum,
        far_term,
    )
    near_back = across(near_term)
    other_back = within(other_sum)
    (own_term,) = call(gather_text, [term], 128 * dot, own_term, second_back)
    own_sum, loss = call(
        gather_images, [term, spec(1, rows, F32)], 64 * dot, own_sum, ahead_back, after=(own_term,)
    )
    (own_term,) = call(
        gather_text, [term], 32 * dot, own_term, near_back, after=(own_sum,)
    )
    grad_student, grad_text, loss = call(
        finish,
        [term, term, jax.ShapeDtypeStruct((rows,), F32)],
        0,
        own_sum,
        loss,
        own_term,
        other_back,
    )
    return grad_student, grad_text, loss


def solution(mesh):
    return jax.shard_map(
        shards,
        mesh=mesh,
        in_specs=(P("dp", None), P("dp", None), P("dp", None), P("dp")),
        out_specs=(P("dp", None), P("dp", None), P("dp")),
        check_vma=False,
    )
```

```python
import jax
import jax.numpy as jnp
from jax import lax
from jax.experimental import pallas as pl
from jax.experimental.pallas import tpu as pltpu
from jax.sharding import PartitionSpec as P

SOFTMAX_TEMP_VALUE = 4.0
LOGIT_BIAS = -3.0
WINDOW = 7
DIGIT = 32.0
LANES = 128
EXTRA = 16

BF16 = jnp.bfloat16
F32 = jnp.float32


def moved(value, even, odd):
    length = lax.axis_size("dp")
    return lax.ppermute(
        value, "dp", [(i, (i + (odd if i % 2 else even)) % length) for i in range(length)]
    )


def within(value):
    return moved(value, 1, -1)


def across(value):
    return moved(value, -1, 1)


def onward(value):
    return moved(value, 2, -2)


def back(value):
    return moved(value, -2, 2)


def call(body, out_shape, flops, *args, after=()):
    count = len(args)

    def ordered(*refs):
        body(*refs[:count], *refs[count + len(after) :])

    in_bytes = sum(a.size * a.dtype.itemsize for a in args)
    out_bytes = sum(o.size * o.dtype.itemsize for o in out_shape)
    return pl.pallas_call(
        ordered,
        out_shape=out_shape,
        in_specs=[pl.BlockSpec(memory_space=pltpu.VMEM)] * count
        + [pl.BlockSpec(memory_space=pl.ANY)] * len(after),
        out_specs=[pl.BlockSpec(memory_space=pltpu.VMEM)] * len(out_shape),
        compiler_params=pltpu.CompilerParams(vmem_limit_bytes=40 * 1024 * 1024),
        cost_estimate=pl.CostEstimate(
            flops=flops, bytes_accessed=in_bytes + out_bytes, transcendentals=0
        ),
    )(*args, *after)


def spread(first, second):
    tiles = [
        row[:, k : k + LANES] for row in (first, second) for k in range(0, row.shape[1], LANES)
    ]
    place = lax.broadcasted_iota(jnp.int32, (EXTRA, LANES), 0)
    out = jnp.zeros((EXTRA, LANES), F32)
    for k, tile in enumerate(tiles):
        out = jnp.where(place == k, tile, out)
    return out.astype(BF16)


def gathered(ref, start, rows):
    tiles = ref[start:, :].astype(F32)
    count = rows // LANES
    first = jnp.concatenate([tiles[k : k + 1, :] for k in range(count)], axis=1)
    second = jnp.concatenate([tiles[k : k + 1, :] for k in range(count, 2 * count)], axis=1)
    return first, second


def digits(species):
    ids = species.reshape(1, species.shape[0]).astype(F32)
    high = jnp.floor(ids / DIGIT)
    return spread(high, ids - high * DIGIT)


def ids_of(ref, rows):
    high, low = gathered(ref, ref.shape[0] - EXTRA, rows)
    return high * DIGIT + low


def put(out_ref, start, value):
    rows = value.shape[0]
    for k in range(value.shape[1] // LANES):
        out_ref[start + k * rows : start + (k + 1) * rows, :] = value[:, k * LANES : (k + 1) * LANES]


def taken(ref, start, rows, width):
    count = width // LANES
    tiles = [ref[start + k * rows : start + (k + 1) * rows, :] for k in range(count)]
    return jnp.concatenate(tiles, axis=1)


def pack_text(text_ref, species_ref, out_ref):
    put(out_ref, 0, text_ref[...])
    out_ref[out_ref.shape[0] - EXTRA :, :] = digits(species_ref[...])


def pack_images(student_ref, teacher_ref, species_ref, text_ref, out_ref, teacher_out, text_out):
    text_out[...] = text_ref[...]
    rows, width = student_ref.shape
    ids = digits(species_ref[...])
    put(out_ref, 0, student_ref[...])
    put(out_ref, rows * width // LANES, teacher_ref[...])
    out_ref[out_ref.shape[0] - EXTRA :, :] = ids
    put(teacher_out, 0, teacher_ref[...])
    teacher_out[teacher_out.shape[0] - EXTRA :, :] = ids


def pair(student, teacher, ids, text, text_ids):
    rows, width = student.shape
    half_scale = 0.5 * SOFTMAX_TEMP_VALUE / float(width) ** 0.5
    contract = (((1,), (1,)), ((), ()))
    half_z = (
        lax.dot_general(student, text, contract, preferred_element_type=F32) * half_scale
        + 0.5 * LOGIT_BIAS
    )
    half_w = (
        lax.dot_general(teacher, text, contract, preferred_element_type=F32) * half_scale
        + 0.5 * LOGIT_BIAS
    )
    column = jnp.transpose(jnp.broadcast_to(ids, (LANES, rows)))
    column = jnp.concatenate([column] * (rows // LANES), axis=1)
    shift = jnp.where(column == text_ids, 0.75, 0.25)
    target = 0.25 * jnp.tanh(half_w) + shift
    tanh_z = jnp.tanh(half_z)
    slope = (0.5 * tanh_z + 0.5) - target
    z = half_z + half_z
    loss = (jnp.maximum(z, 0.0) - target * z) - jnp.log(0.5 * jnp.abs(tanh_z) + 0.5)
    folded = sum(loss[:, k : k + LANES] for k in range(0, rows, LANES))
    return slope.astype(BF16), folded


def text_term(slope, student):
    return lax.dot_general(slope, student, (((0,), (0,)), ((), ())), preferred_element_type=F32)


def unpacked(ref, rows):
    width = (ref.shape[0] - EXTRA) * LANES // rows
    return taken(ref, 0, rows, width), ids_of(ref, rows)


def both_images(ref, rows):
    size = (ref.shape[0] - EXTRA) // 2
    width = size * LANES // rows
    return taken(ref, 0, rows, width), taken(ref, size, rows, width), ids_of(ref, rows)


def block(images, texts):
    student, teacher, ids = images
    slope, folded = pair(student, teacher, ids, *texts)
    grad = jnp.dot(slope, texts[0], preferred_element_type=F32)
    return grad, folded, text_term(slope, student)


def two_blocks(images, texts, sums_in, sums_out):
    rows, width = texts[0].shape
    pairs = [pair(student, teacher, ids, *texts) for student, teacher, ids in images]
    slope = jnp.concatenate([slope for slope, _ in pairs], axis=0)
    grad = jnp.dot(slope, texts[0], preferred_element_type=F32)
    for k, (was, out) in enumerate(zip(sums_in, sums_out)):
        out[:, :width] = was[:, :width] + grad[k * rows : (k + 1) * rows, :]
        out[:, width:] = was[:, width:] + pairs[k][1]
    return text_term(slope, jnp.concatenate([student for student, _, _ in images], axis=0))


def own_first(own_ref, text_ref, sums_ref, term_ref):
    rows, width = term_ref.shape
    images = both_images(own_ref, rows)
    sums_ref[:, :width], sums_ref[:, width:], term_ref[...] = block(images, unpacked(text_ref, rows))


def other_first(other_ref, text_ref, term_in, sums_ref, term_ref):
    rows, width = term_ref.shape
    images = both_images(other_ref, rows)
    sums_ref[:, :width], sums_ref[:, width:], term = block(images, unpacked(text_ref, rows))
    term_ref[...] = term_in[...] + term


def both(own_ref, other_ref, text_ref, own_in, other_in, own_out, other_out, term_ref):
    rows = term_ref.shape[0]
    images = [both_images(ref, rows) for ref in (own_ref, other_ref)]
    sums_in, sums_out = (own_in, other_in), (own_out, other_out)
    term = two_blocks(images, unpacked(text_ref, rows), sums_in, sums_out)
    term_ref[...] = term.astype(term_ref.dtype)


def both_near(
    own_ref, other_ref, text_ref, own_in, other_in, term_in, own_out, other_out, term_ref
):
    rows = term_ref.shape[0]
    images = [both_images(ref, rows) for ref in (own_ref, other_ref)]
    sums_in, sums_out = (own_in, other_in), (own_out, other_out)
    term = two_blocks(images, unpacked(text_ref, rows), sums_in, sums_out)
    term_ref[...] = (term_in[...] + term).astype(term_ref.dtype)


def loss_row(folded):
    return jnp.sum(jnp.transpose(folded), axis=0, keepdims=True)


def ahead_near(student_ref, teacher_ref, near_ref, ahead_out, term_ref):
    rows = term_ref.shape[0]
    images = (student_ref[...], *unpacked(teacher_ref, rows))
    grad, folded, term_ref[...] = block(images, unpacked(near_ref, rows))
    put(ahead_out, 0, grad.astype(BF16))
    loss = loss_row(folded)
    high = loss.astype(BF16).astype(F32)
    ahead_out[ahead_out.shape[0] - EXTRA :, :] = spread(high, loss - high)


def gather_text(own_ref, second_ref, term_ref):
    term_ref[...] = own_ref[...] + second_ref[...].astype(F32)


def gather_images(own_ref, ahead_ref, sums_ref, loss_ref):
    rows, width = own_ref.shape[0], own_ref.shape[1] - LANES
    sums_ref[...] = own_ref[:, :width] + taken(ahead_ref, 0, rows, width).astype(F32)
    high, low = gathered(ahead_ref, ahead_ref.shape[0] - EXTRA, rows)
    loss_ref[...] = loss_row(own_ref[:, width:]) + high + low


def finish(sums_in, loss_in, term_in, other_ref, grad_ref, text_ref, loss_ref):
    rows, width = grad_ref.shape
    scale = SOFTMAX_TEMP_VALUE / float(width) ** 0.5
    text_ref[...] = term_in[...] * scale
    grad_ref[...] = (sums_in[...] + other_ref[:, :width]) * scale
    loss = loss_in[...] + loss_row(other_ref[:, width:])
    loss_ref[...] = (loss / float(WINDOW * rows)).reshape(rows)


def shards(student_image_vectors, teacher_emb, text_emb, species):
    rows, width = text_emb.shape
    dot = 2 * rows * rows * width

    def spec(n, m, dtype):
        return jax.ShapeDtypeStruct((n, m), dtype)

    sums = spec(rows, width + LANES, F32)
    term = spec(rows, width, F32)
    sent = spec(rows, width, BF16)
    packed = spec(rows * width // LANES + EXTRA, LANES, BF16)
    ahead_student = back(student_image_vectors)
    (text,) = call(pack_text, [packed], 0, text_emb, species)
    second = onward(text)
    images, teacher, text_again = call(
        pack_images,
        [spec(2 * rows * width // LANES + EXTRA, LANES, BF16), packed, packed],
        0,
        student_image_vectors,
        teacher_emb,
        species,
        text,
    )
    near = across(text_again)
    other = within(images)
    ahead_teacher = back(teacher)
    own_sum, own_term = call(
        own_first, [sums, term], 64 * dot, images, text, after=(ahead_student,)
    )
    other_sum, own_term = call(other_first, [sums, term], 16 * dot, other, text, own_term)
    own_sum, other_sum, second_term = call(
        both, [sums, sums, sent], 16 * dot, images, other, second, own_sum, other_sum
    )
    second_back = back(second_term)
    ahead_sum, far_term = call(
        ahead_near,
        [packed, term],
        4 * dot,
        ahead_student,
        ahead_teacher,
        near,
        after=(second_term,),
    )
    ahead_back = onward(ahead_sum)
    own_sum, other_sum, near_term = call(
        both_near,
        [sums, sums, sent],
        0 * dot,
        images,
        other,
        near,
        own_sum,
        other_sum,
        far_term,
    )
    near_back = across(near_term)
    other_back = within(other_sum)
    (own_term,) = call(gather_text, [term], 128 * dot, own_term, second_back)
    own_sum, loss = call(
        gather_images, [term, spec(1, rows, F32)], 64 * dot, own_sum, ahead_back, after=(own_term,)
    )
    (own_term,) = call(
        gather_text, [term], 32 * dot, own_term, near_back, after=(own_sum,)
    )
    grad_student, grad_text, loss = call(
        finish,
        [term, term, jax.ShapeDtypeStruct((rows,), F32)],
        0,
        own_sum,
        loss,
        own_term,
        other_back,
    )
    return grad_student, grad_text, loss


def solution(mesh):
    return jax.shard_map(
        shards,
        mesh=mesh,
        in_specs=(P("dp", None), P("dp", None), P("dp", None), P("dp")),
        out_specs=(P("dp", None), P("dp", None), P("dp")),
        check_vma=False,
    )
```

```python
import jax
import jax.numpy as jnp
from jax import lax
from jax.experimental import pallas as pl
from jax.experimental.pallas import tpu as pltpu
from jax.sharding import PartitionSpec as P

SOFTMAX_TEMP_VALUE = 4.0
LOGIT_BIAS = -3.0
WINDOW = 7
DIGIT = 32.0
LANES = 128
EXTRA = 16

BF16 = jnp.bfloat16
F32 = jnp.float32


def moved(value, even, odd):
    length = lax.axis_size("dp")
    return lax.ppermute(
        value, "dp", [(i, (i + (odd if i % 2 else even)) % length) for i in range(length)]
    )


def within(value):
    return moved(value, 1, -1)


def across(value):
    return moved(value, -1, 1)


def onward(value):
    return moved(value, 2, -2)


def back(value):
    return moved(value, -2, 2)


def call(body, out_shape, flops, *args, after=()):
    count = len(args)

    def ordered(*refs):
        body(*refs[:count], *refs[count + len(after) :])

    in_bytes = sum(a.size * a.dtype.itemsize for a in args)
    out_bytes = sum(o.size * o.dtype.itemsize for o in out_shape)
    return pl.pallas_call(
        ordered,
        out_shape=out_shape,
        in_specs=[pl.BlockSpec(memory_space=pltpu.VMEM)] * count
        + [pl.BlockSpec(memory_space=pl.ANY)] * len(after),
        out_specs=[pl.BlockSpec(memory_space=pltpu.VMEM)] * len(out_shape),
        compiler_params=pltpu.CompilerParams(vmem_limit_bytes=40 * 1024 * 1024),
        cost_estimate=pl.CostEstimate(
            flops=flops, bytes_accessed=in_bytes + out_bytes, transcendentals=0
        ),
    )(*args, *after)


def spread(first, second):
    tiles = [
        row[:, k : k + LANES] for row in (first, second) for k in range(0, row.shape[1], LANES)
    ]
    place = lax.broadcasted_iota(jnp.int32, (EXTRA, LANES), 0)
    out = jnp.zeros((EXTRA, LANES), F32)
    for k, tile in enumerate(tiles):
        out = jnp.where(place == k, tile, out)
    return out.astype(BF16)


def gathered(ref, start, rows):
    tiles = ref[start:, :].astype(F32)
    count = rows // LANES
    first = jnp.concatenate([tiles[k : k + 1, :] for k in range(count)], axis=1)
    second = jnp.concatenate([tiles[k : k + 1, :] for k in range(count, 2 * count)], axis=1)
    return first, second


def digits(species):
    ids = species.reshape(1, species.shape[0]).astype(F32)
    high = jnp.floor(ids / DIGIT)
    return spread(high, ids - high * DIGIT)


def ids_of(ref, rows):
    high, low = gathered(ref, ref.shape[0] - EXTRA, rows)
    return high * DIGIT + low


def put(out_ref, start, value):
    rows = value.shape[0]
    for k in range(value.shape[1] // LANES):
        out_ref[start + k * rows : start + (k + 1) * rows, :] = value[:, k * LANES : (k + 1) * LANES]


def taken(ref, start, rows, width):
    count = width // LANES
    tiles = [ref[start + k * rows : start + (k + 1) * rows, :] for k in range(count)]
    return jnp.concatenate(tiles, axis=1)


def pack_text(text_ref, species_ref, out_ref):
    put(out_ref, 0, text_ref[...])
    out_ref[out_ref.shape[0] - EXTRA :, :] = digits(species_ref[...])


def pack_images(student_ref, teacher_ref, species_ref, text_ref, out_ref, teacher_out, text_out):
    text_out[...] = text_ref[...]
    rows, width = student_ref.shape
    ids = digits(species_ref[...])
    put(out_ref, 0, student_ref[...])
    put(out_ref, rows * width // LANES, teacher_ref[...])
    out_ref[out_ref.shape[0] - EXTRA :, :] = ids
    put(teacher_out, 0, teacher_ref[...])
    teacher_out[teacher_out.shape[0] - EXTRA :, :] = ids


def pair(student, teacher, ids, text, text_ids):
    rows, width = student.shape
    half_scale = 0.5 * SOFTMAX_TEMP_VALUE / float(width) ** 0.5
    contract = (((1,), (1,)), ((), ()))
    half_z = (
        lax.dot_general(student, text, contract, preferred_element_type=F32) * half_scale
        + 0.5 * LOGIT_BIAS
    )
    half_w = (
        lax.dot_general(teacher, text, contract, preferred_element_type=F32) * half_scale
        + 0.5 * LOGIT_BIAS
    )
    column = jnp.transpose(jnp.broadcast_to(ids, (LANES, rows)))
    column = jnp.concatenate([column] * (rows // LANES), axis=1)
    shift = jnp.where(column == text_ids, 0.75, 0.25)
    target = 0.25 * jnp.tanh(half_w) + shift
    tanh_z = jnp.tanh(half_z)
    slope = (0.5 * tanh_z + 0.5) - target
    z = half_z + half_z
    loss = (jnp.maximum(z, 0.0) - target * z) - jnp.log(0.5 * jnp.abs(tanh_z) + 0.5)
    folded = sum(loss[:, k : k + LANES] for k in range(0, rows, LANES))
    return slope.astype(BF16), folded


def text_term(slope, student):
    return lax.dot_general(slope, student, (((0,), (0,)), ((), ())), preferred_element_type=F32)


def unpacked(ref, rows):
    width = (ref.shape[0] - EXTRA) * LANES // rows
    return taken(ref, 0, rows, width), ids_of(ref, rows)


def both_images(ref, rows):
    size = (ref.shape[0] - EXTRA) // 2
    width = size * LANES // rows
    return taken(ref, 0, rows, width), taken(ref, size, rows, width), ids_of(ref, rows)


def block(images, texts):
    student, teacher, ids = images
    slope, folded = pair(student, teacher, ids, *texts)
    grad = jnp.dot(slope, texts[0], preferred_element_type=F32)
    return grad, folded, text_term(slope, student)


def two_blocks(images, texts, sums_in, sums_out):
    rows, width = texts[0].shape
    pairs = [pair(student, teacher, ids, *texts) for student, teacher, ids in images]
    slope = jnp.concatenate([slope for slope, _ in pairs], axis=0)
    grad = jnp.dot(slope, texts[0], preferred_element_type=F32)
    for k, (was, out) in enumerate(zip(sums_in, sums_out)):
        out[:, :width] = was[:, :width] + grad[k * rows : (k + 1) * rows, :]
        out[:, width:] = was[:, width:] + pairs[k][1]
    return text_term(slope, jnp.concatenate([student for student, _, _ in images], axis=0))


def own_first(own_ref, text_ref, sums_ref, term_ref):
    rows, width = term_ref.shape
    images = both_images(own_ref, rows)
    sums_ref[:, :width], sums_ref[:, width:], term_ref[...] = block(images, unpacked(text_ref, rows))


def other_first(other_ref, text_ref, term_in, sums_ref, term_ref):
    rows, width = term_ref.shape
    images = both_images(other_ref, rows)
    sums_ref[:, :width], sums_ref[:, width:], term = block(images, unpacked(text_ref, rows))
    term_ref[...] = term_in[...] + term


def both(own_ref, other_ref, text_ref, own_in, other_in, own_out, other_out, term_ref):
    rows = term_ref.shape[0]
    images = [both_images(ref, rows) for ref in (own_ref, other_ref)]
    sums_in, sums_out = (own_in, other_in), (own_out, other_out)
    term = two_blocks(images, unpacked(text_ref, rows), sums_in, sums_out)
    term_ref[...] = term.astype(term_ref.dtype)


def loss_row(folded):
    return jnp.sum(jnp.transpose(folded), axis=0, keepdims=True)


def ahead_near(student_ref, teacher_ref, near_ref, term_in, ahead_out, term_ref):
    rows = term_ref.shape[0]
    images = (student_ref[...], *unpacked(teacher_ref, rows))
    grad, folded, term = block(images, unpacked(near_ref, rows))
    term_ref[...] = (term_in[...] + term).astype(term_ref.dtype)
    put(ahead_out, 0, grad.astype(BF16))
    loss = loss_row(folded)
    high = loss.astype(BF16).astype(F32)
    ahead_out[ahead_out.shape[0] - EXTRA :, :] = spread(high, loss - high)


def gather_text(own_ref, second_ref, term_ref):
    term_ref[...] = own_ref[...] + second_ref[...].astype(F32)


def gather_images(own_ref, ahead_ref, sums_ref, loss_ref):
    rows, width = own_ref.shape[0], own_ref.shape[1] - LANES
    sums_ref[...] = own_ref[:, :width] + taken(ahead_ref, 0, rows, width).astype(F32)
    high, low = gathered(ahead_ref, ahead_ref.shape[0] - EXTRA, rows)
    loss_ref[...] = loss_row(own_ref[:, width:]) + high + low


def finish(sums_in, loss_in, term_in, other_ref, grad_ref, text_ref, loss_ref):
    rows, width = grad_ref.shape
    scale = SOFTMAX_TEMP_VALUE / float(width) ** 0.5
    text_ref[...] = term_in[...] * scale
    grad_ref[...] = (sums_in[...] + other_ref[:, :width]) * scale
    loss = loss_in[...] + loss_row(other_ref[:, width:])
    loss_ref[...] = (loss / float(WINDOW * rows)).reshape(rows)


def shards(student_image_vectors, teacher_emb, text_emb, species):
    rows, width = text_emb.shape
    dot = 2 * rows * rows * width

    def spec(n, m, dtype):
        return jax.ShapeDtypeStruct((n, m), dtype)

    sums = spec(rows, width + LANES, F32)
    term = spec(rows, width, F32)
    sent = spec(rows, width, BF16)
    packed = spec(rows * width // LANES + EXTRA, LANES, BF16)
    ahead_student = back(student_image_vectors)
    (text,) = call(pack_text, [packed], 0, text_emb, species)
    second = onward(text)
    images, teacher, text_again = call(
        pack_images,
        [spec(2 * rows * width // LANES + EXTRA, LANES, BF16), packed, packed],
        0,
        student_image_vectors,
        teacher_emb,
        species,
        text,
    )
    near = across(text_again)
    other = within(images)
    ahead_teacher = back(teacher)
    own_sum, own_term = call(
        own_first, [sums, term], 64 * dot, images, text, after=(ahead_student,)
    )
    other_sum, own_term = call(other_first, [sums, term], 16 * dot, other, text, own_term)
    own_sum, other_sum, second_term = call(
        both, [sums, sums, sent], 16 * dot, images, other, second, own_sum, other_sum
    )
    second_back = back(second_term)
    own_sum, other_sum, near_term = call(
        both, [sums, sums, term], 0 * dot, images, other, near, own_sum, other_sum
    )
    ahead_sum, near_term = call(
        ahead_near, [packed, sent], 0 * dot, ahead_student, ahead_teacher, near, near_term
    )
    ahead_back = onward(ahead_sum)
    near_back = across(near_term)
    other_back = within(other_sum)
    (own_term,) = call(gather_text, [term], 128 * dot, own_term, second_back)
    own_sum, loss = call(
        gather_images, [term, spec(1, rows, F32)], 64 * dot, own_sum, ahead_back, after=(own_term,)
    )
    (own_term,) = call(
        gather_text, [term], 32 * dot, own_term, near_back, after=(own_sum,)
    )
    grad_student, grad_text, loss = call(
        finish,
        [term, term, jax.ShapeDtypeStruct((rows,), F32)],
        0,
        own_sum,
        loss,
        own_term,
        other_back,
    )
    return grad_student, grad_text, loss


def solution(mesh):
    return jax.shard_map(
        shards,
        mesh=mesh,
        in_specs=(P("dp", None), P("dp", None), P("dp", None), P("dp")),
        out_specs=(P("dp", None), P("dp", None), P("dp")),
        check_vma=False,
    )
```

```python
import jax
import jax.numpy as jnp
from jax import lax
from jax.experimental import pallas as pl
from jax.experimental.pallas import tpu as pltpu
from jax.sharding import PartitionSpec as P

SOFTMAX_TEMP_VALUE = 4.0
LOGIT_BIAS = -3.0
WINDOW = 7
DIGIT = 32.0
LANES = 128
EXTRA = 16

BF16 = jnp.bfloat16
F32 = jnp.float32


def moved(value, even, odd):
    length = lax.axis_size("dp")
    return lax.ppermute(
        value, "dp", [(i, (i + (odd if i % 2 else even)) % length) for i in range(length)]
    )


def within(value):
    return moved(value, 1, -1)


def across(value):
    return moved(value, -1, 1)


def onward(value):
    return moved(value, 2, -2)


def back(value):
    return moved(value, -2, 2)


def call(body, out_shape, flops, *args, after=()):
    count = len(args)

    def ordered(*refs):
        body(*refs[:count], *refs[count + len(after) :])

    in_bytes = sum(a.size * a.dtype.itemsize for a in args)
    out_bytes = sum(o.size * o.dtype.itemsize for o in out_shape)
    return pl.pallas_call(
        ordered,
        out_shape=out_shape,
        in_specs=[pl.BlockSpec(memory_space=pltpu.VMEM)] * count
        + [pl.BlockSpec(memory_space=pl.ANY)] * len(after),
        out_specs=[pl.BlockSpec(memory_space=pltpu.VMEM)] * len(out_shape),
        compiler_params=pltpu.CompilerParams(vmem_limit_bytes=40 * 1024 * 1024),
        cost_estimate=pl.CostEstimate(
            flops=flops, bytes_accessed=in_bytes + out_bytes, transcendentals=0
        ),
    )(*args, *after)


def spread(first, second):
    tiles = [
        row[:, k : k + LANES] for row in (first, second) for k in range(0, row.shape[1], LANES)
    ]
    place = lax.broadcasted_iota(jnp.int32, (EXTRA, LANES), 0)
    out = jnp.zeros((EXTRA, LANES), F32)
    for k, tile in enumerate(tiles):
        out = jnp.where(place == k, tile, out)
    return out.astype(BF16)


def gathered(ref, start, rows):
    tiles = ref[start:, :].astype(F32)
    count = rows // LANES
    first = jnp.concatenate([tiles[k : k + 1, :] for k in range(count)], axis=1)
    second = jnp.concatenate([tiles[k : k + 1, :] for k in range(count, 2 * count)], axis=1)
    return first, second


def digits(species):
    ids = species.reshape(1, species.shape[0]).astype(F32)
    high = jnp.floor(ids / DIGIT)
    return spread(high, ids - high * DIGIT)


def ids_of(ref, rows):
    high, low = gathered(ref, ref.shape[0] - EXTRA, rows)
    return high * DIGIT + low


def put(out_ref, start, value):
    rows = value.shape[0]
    for k in range(value.shape[1] // LANES):
        out_ref[start + k * rows : start + (k + 1) * rows, :] = value[:, k * LANES : (k + 1) * LANES]


def taken(ref, start, rows, width):
    count = width // LANES
    tiles = [ref[start + k * rows : start + (k + 1) * rows, :] for k in range(count)]
    return jnp.concatenate(tiles, axis=1)


def pack_text(text_ref, species_ref, out_ref):
    put(out_ref, 0, text_ref[...])
    out_ref[out_ref.shape[0] - EXTRA :, :] = digits(species_ref[...])


def pack_images(student_ref, teacher_ref, species_ref, text_ref, out_ref, teacher_out, text_out):
    text_out[...] = text_ref[...]
    rows, width = student_ref.shape
    ids = digits(species_ref[...])
    put(out_ref, 0, student_ref[...])
    put(out_ref, rows * width // LANES, teacher_ref[...])
    out_ref[out_ref.shape[0] - EXTRA :, :] = ids
    put(teacher_out, 0, teacher_ref[...])
    teacher_out[teacher_out.shape[0] - EXTRA :, :] = ids


def pair(student, teacher, ids, text, text_ids):
    rows, width = student.shape
    half_scale = 0.5 * SOFTMAX_TEMP_VALUE / float(width) ** 0.5
    contract = (((1,), (1,)), ((), ()))
    half_z = (
        lax.dot_general(student, text, contract, preferred_element_type=F32) * half_scale
        + 0.5 * LOGIT_BIAS
    )
    half_w = (
        lax.dot_general(teacher, text, contract, preferred_element_type=F32) * half_scale
        + 0.5 * LOGIT_BIAS
    )
    column = jnp.transpose(jnp.broadcast_to(ids, (LANES, rows)))
    column = jnp.concatenate([column] * (rows // LANES), axis=1)
    shift = jnp.where(column == text_ids, 0.75, 0.25)
    target = 0.25 * jnp.tanh(half_w) + shift
    tanh_z = jnp.tanh(half_z)
    slope = (0.5 * tanh_z + 0.5) - target
    z = half_z + half_z
    loss = (jnp.maximum(z, 0.0) - target * z) - jnp.log(0.5 * jnp.abs(tanh_z) + 0.5)
    folded = sum(loss[:, k : k + LANES] for k in range(0, rows, LANES))
    return slope.astype(BF16), folded


def text_term(slope, student):
    return lax.dot_general(slope, student, (((0,), (0,)), ((), ())), preferred_element_type=F32)


def unpacked(ref, rows):
    width = (ref.shape[0] - EXTRA) * LANES // rows
    return taken(ref, 0, rows, width), ids_of(ref, rows)


def both_images(ref, rows):
    size = (ref.shape[0] - EXTRA) // 2
    width = size * LANES // rows
    return taken(ref, 0, rows, width), taken(ref, size, rows, width), ids_of(ref, rows)


def block(images, texts):
    student, teacher, ids = images
    slope, folded = pair(student, teacher, ids, *texts)
    grad = jnp.dot(slope, texts[0], preferred_element_type=F32)
    return grad, folded, text_term(slope, student)


def two_blocks(images, texts, sums_in, sums_out):
    rows, width = texts[0].shape
    pairs = [pair(student, teacher, ids, *texts) for student, teacher, ids in images]
    slope = jnp.concatenate([slope for slope, _ in pairs], axis=0)
    grad = jnp.dot(slope, texts[0], preferred_element_type=F32)
    for k, (was, out) in enumerate(zip(sums_in, sums_out)):
        out[:, :width] = was[:, :width] + grad[k * rows : (k + 1) * rows, :]
        out[:, width:] = was[:, width:] + pairs[k][1]
    return text_term(slope, jnp.concatenate([student for student, _, _ in images], axis=0))


def own_first(own_ref, text_ref, sums_ref, term_ref):
    rows, width = term_ref.shape
    images = both_images(own_ref, rows)
    sums_ref[:, :width], sums_ref[:, width:], term_ref[...] = block(images, unpacked(text_ref, rows))


def other_first(other_ref, text_ref, term_in, sums_ref, term_ref):
    rows, width = term_ref.shape
    images = both_images(other_ref, rows)
    sums_ref[:, :width], sums_ref[:, width:], term = block(images, unpacked(text_ref, rows))
    term_ref[...] = term_in[...] + term


def both(own_ref, other_ref, text_ref, own_in, other_in, own_out, other_out, term_ref):
    rows = term_ref.shape[0]
    images = [both_images(ref, rows) for ref in (own_ref, other_ref)]
    sums_in, sums_out = (own_in, other_in), (own_out, other_out)
    term = two_blocks(images, unpacked(text_ref, rows), sums_in, sums_out)
    term_ref[...] = term.astype(term_ref.dtype)


def loss_row(folded):
    return jnp.sum(jnp.transpose(folded), axis=0, keepdims=True)


def ahead_near(student_ref, teacher_ref, near_ref, term_in, ahead_out, term_ref):
    rows = term_ref.shape[0]
    images = (student_ref[...], *unpacked(teacher_ref, rows))
    grad, folded, term = block(images, unpacked(near_ref, rows))
    term_ref[...] = (term_in[...] + term).astype(term_ref.dtype)
    put(ahead_out, 0, grad.astype(BF16))
    loss = loss_row(folded)
    high = loss.astype(BF16).astype(F32)
    ahead_out[ahead_out.shape[0] - EXTRA :, :] = spread(high, loss - high)


def gather_text(own_ref, second_ref, term_ref):
    term_ref[...] = own_ref[...] + second_ref[...].astype(F32)


def gather_images(own_ref, ahead_ref, sums_ref, loss_ref):
    rows, width = own_ref.shape[0], own_ref.shape[1] - LANES
    sums_ref[...] = own_ref[:, :width] + taken(ahead_ref, 0, rows, width).astype(F32)
    high, low = gathered(ahead_ref, ahead_ref.shape[0] - EXTRA, rows)
    loss_ref[...] = loss_row(own_ref[:, width:]) + high + low


def finish_images(sums_in, loss_in, other_ref, grad_ref, loss_ref, done_ref):
    rows, width = grad_ref.shape
    scale = SOFTMAX_TEMP_VALUE / float(width) ** 0.5
    grad_ref[...] = (sums_in[...] + other_ref[:, :width]) * scale
    loss = loss_in[...] + loss_row(other_ref[:, width:])
    loss_ref[...] = (loss / float(WINDOW * rows)).reshape(rows)
    done_ref[...] = jnp.zeros_like(done_ref)


def finish_text(own_ref, near_ref, out_ref):
    scale = SOFTMAX_TEMP_VALUE / float(out_ref.shape[1]) ** 0.5
    out_ref[...] = (own_ref[...] + near_ref[...].astype(F32)) * scale


def shards(student_image_vectors, teacher_emb, text_emb, species):
    rows, width = text_emb.shape
    dot = 2 * rows * rows * width

    def spec(n, m, dtype):
        return jax.ShapeDtypeStruct((n, m), dtype)

    sums = spec(rows, width + LANES, F32)
    term = spec(rows, width, F32)
    sent = spec(rows, width, BF16)
    packed = spec(rows * width // LANES + EXTRA, LANES, BF16)
    ahead_student = back(student_image_vectors)
    (text,) = call(pack_text, [packed], 0, text_emb, species)
    second = onward(text)
    images, teacher, text_again = call(
        pack_images,
        [spec(2 * rows * width // LANES + EXTRA, LANES, BF16), packed, packed],
        0,
        student_image_vectors,
        teacher_emb,
        species,
        text,
    )
    near = across(text_again)
    other = within(images)
    ahead_teacher = back(teacher)
    own_sum, own_term = call(
        own_first, [sums, term], 64 * dot, images, text, after=(ahead_student,)
    )
    other_sum, own_term = call(other_first, [sums, term], 16 * dot, other, text, own_term)
    own_sum, other_sum, second_term = call(
        both, [sums, sums, sent], 16 * dot, images, other, second, own_sum, other_sum
    )
    second_back = back(second_term)
    own_sum, other_sum, near_term = call(
        both, [sums, sums, term], 0 * dot, images, other, near, own_sum, other_sum
    )
    ahead_sum, near_term = call(
        ahead_near, [packed, sent], 0 * dot, ahead_student, ahead_teacher, near, near_term
    )
    ahead_back = onward(ahead_sum)
    near_back = across(near_term)
    other_back = within(other_sum)
    (own_term,) = call(gather_text, [term], 128 * dot, own_term, second_back)
    own_sum, loss = call(
        gather_images, [term, spec(1, rows, F32)], 64 * dot, own_sum, ahead_back, after=(own_term,)
    )
    grad_student, loss, done = call(
        finish_images,
        [term, jax.ShapeDtypeStruct((rows,), F32), spec(8, LANES, F32)],
        0,
        own_sum,
        loss,
        other_back,
    )
    (grad_text,) = call(finish_text, [term], 0, own_term, near_back, after=(done,))
    return grad_student, grad_text, loss


def solution(mesh):
    return jax.shard_map(
        shards,
        mesh=mesh,
        in_specs=(P("dp", None), P("dp", None), P("dp", None), P("dp")),
        out_specs=(P("dp", None), P("dp", None), P("dp")),
        check_vma=False,
    )
```

```python
import jax
import jax.numpy as jnp
from jax import lax
from jax.experimental import pallas as pl
from jax.experimental.pallas import tpu as pltpu
from jax.sharding import PartitionSpec as P

SOFTMAX_TEMP_VALUE = 4.0
LOGIT_BIAS = -3.0
WINDOW = 7
DIGIT = 32.0
LANES = 128
EXTRA = 16

BF16 = jnp.bfloat16
F32 = jnp.float32


def moved(value, even, odd):
    length = lax.axis_size("dp")
    return lax.ppermute(
        value, "dp", [(i, (i + (odd if i % 2 else even)) % length) for i in range(length)]
    )


def within(value):
    return moved(value, 1, -1)


def across(value):
    return moved(value, -1, 1)


def onward(value):
    return moved(value, 2, -2)


def back(value):
    return moved(value, -2, 2)


def call(body, out_shape, flops, *args, after=()):
    count = len(args)

    def ordered(*refs):
        body(*refs[:count], *refs[count + len(after) :])

    in_bytes = sum(a.size * a.dtype.itemsize for a in args)
    out_bytes = sum(o.size * o.dtype.itemsize for o in out_shape)
    return pl.pallas_call(
        ordered,
        out_shape=out_shape,
        in_specs=[pl.BlockSpec(memory_space=pltpu.VMEM)] * count
        + [pl.BlockSpec(memory_space=pl.ANY)] * len(after),
        out_specs=[pl.BlockSpec(memory_space=pltpu.VMEM)] * len(out_shape),
        compiler_params=pltpu.CompilerParams(vmem_limit_bytes=40 * 1024 * 1024),
        cost_estimate=pl.CostEstimate(
            flops=flops, bytes_accessed=in_bytes + out_bytes, transcendentals=0
        ),
    )(*args, *after)


def spread(first, second):
    tiles = [
        row[:, k : k + LANES] for row in (first, second) for k in range(0, row.shape[1], LANES)
    ]
    place = lax.broadcasted_iota(jnp.int32, (EXTRA, LANES), 0)
    out = jnp.zeros((EXTRA, LANES), F32)
    for k, tile in enumerate(tiles):
        out = jnp.where(place == k, tile, out)
    return out.astype(BF16)


def gathered(ref, start, rows):
    tiles = ref[start:, :].astype(F32)
    count = rows // LANES
    first = jnp.concatenate([tiles[k : k + 1, :] for k in range(count)], axis=1)
    second = jnp.concatenate([tiles[k : k + 1, :] for k in range(count, 2 * count)], axis=1)
    return first, second


def digits(species):
    ids = species.reshape(1, species.shape[0]).astype(F32)
    high = jnp.floor(ids / DIGIT)
    return spread(high, ids - high * DIGIT)


def ids_of(ref, rows):
    high, low = gathered(ref, ref.shape[0] - EXTRA, rows)
    return high * DIGIT + low


def put(out_ref, start, value):
    rows = value.shape[0]
    for k in range(value.shape[1] // LANES):
        out_ref[start + k * rows : start + (k + 1) * rows, :] = value[:, k * LANES : (k + 1) * LANES]


def taken(ref, start, rows, width):
    count = width // LANES
    tiles = [ref[start + k * rows : start + (k + 1) * rows, :] for k in range(count)]
    return jnp.concatenate(tiles, axis=1)


def pack_text(text_ref, species_ref, out_ref):
    put(out_ref, 0, text_ref[...])
    out_ref[out_ref.shape[0] - EXTRA :, :] = digits(species_ref[...])


def first_token(out_ref):
    out_ref[...] = jnp.zeros_like(out_ref)


def pack_images(student_ref, teacher_ref, species_ref, text_ref, out_ref, teacher_out, text_out):
    text_out[...] = text_ref[...]
    rows, width = student_ref.shape
    ids = digits(species_ref[...])
    put(out_ref, 0, student_ref[...])
    put(out_ref, rows * width // LANES, teacher_ref[...])
    out_ref[out_ref.shape[0] - EXTRA :, :] = ids
    put(teacher_out, 0, teacher_ref[...])
    teacher_out[teacher_out.shape[0] - EXTRA :, :] = ids


def pair(student, teacher, ids, text, text_ids):
    rows, width = student.shape
    half_scale = 0.5 * SOFTMAX_TEMP_VALUE / float(width) ** 0.5
    contract = (((1,), (1,)), ((), ()))
    half_z = (
        lax.dot_general(student, text, contract, preferred_element_type=F32) * half_scale
        + 0.5 * LOGIT_BIAS
    )
    half_w = (
        lax.dot_general(teacher, text, contract, preferred_element_type=F32) * half_scale
        + 0.5 * LOGIT_BIAS
    )
    column = jnp.transpose(jnp.broadcast_to(ids, (LANES, rows)))
    column = jnp.concatenate([column] * (rows // LANES), axis=1)
    shift = jnp.where(column == text_ids, 0.75, 0.25)
    target = 0.25 * jnp.tanh(half_w) + shift
    tanh_z = jnp.tanh(half_z)
    slope = (0.5 * tanh_z + 0.5) - target
    z = half_z + half_z
    loss = (jnp.maximum(z, 0.0) - target * z) - jnp.log(0.5 * jnp.abs(tanh_z) + 0.5)
    folded = sum(loss[:, k : k + LANES] for k in range(0, rows, LANES))
    return slope.astype(BF16), folded


def text_term(slope, student):
    return lax.dot_general(slope, student, (((0,), (0,)), ((), ())), preferred_element_type=F32)


def unpacked(ref, rows):
    width = (ref.shape[0] - EXTRA) * LANES // rows
    return taken(ref, 0, rows, width), ids_of(ref, rows)


def both_images(ref, rows):
    size = (ref.shape[0] - EXTRA) // 2
    width = size * LANES // rows
    return taken(ref, 0, rows, width), taken(ref, size, rows, width), ids_of(ref, rows)


def block(images, texts):
    student, teacher, ids = images
    slope, folded = pair(student, teacher, ids, *texts)
    grad = jnp.dot(slope, texts[0], preferred_element_type=F32)
    return grad, folded, text_term(slope, student)


def two_blocks(images, texts, sums_in, sums_out):
    rows, width = texts[0].shape
    pairs = [pair(student, teacher, ids, *texts) for student, teacher, ids in images]
    slope = jnp.concatenate([slope for slope, _ in pairs], axis=0)
    grad = jnp.dot(slope, texts[0], preferred_element_type=F32)
    for k, (was, out) in enumerate(zip(sums_in, sums_out)):
        out[:, :width] = was[:, :width] + grad[k * rows : (k + 1) * rows, :]
        out[:, width:] = was[:, width:] + pairs[k][1]
    return text_term(slope, jnp.concatenate([student for student, _, _ in images], axis=0))


def own_first(own_ref, text_ref, sums_ref, term_ref):
    rows, width = term_ref.shape
    images = both_images(own_ref, rows)
    sums_ref[:, :width], sums_ref[:, width:], term_ref[...] = block(images, unpacked(text_ref, rows))


def other_first(other_ref, text_ref, term_in, sums_ref, term_ref):
    rows, width = term_ref.shape
    images = both_images(other_ref, rows)
    sums_ref[:, :width], sums_ref[:, width:], term = block(images, unpacked(text_ref, rows))
    term_ref[...] = term_in[...] + term


def both(own_ref, other_ref, text_ref, own_in, other_in, own_out, other_out, term_ref):
    rows = term_ref.shape[0]
    images = [both_images(ref, rows) for ref in (own_ref, other_ref)]
    sums_in, sums_out = (own_in, other_in), (own_out, other_out)
    term = two_blocks(images, unpacked(text_ref, rows), sums_in, sums_out)
    term_ref[...] = term.astype(term_ref.dtype)


def loss_row(folded):
    return jnp.sum(jnp.transpose(folded), axis=0, keepdims=True)


def ahead_near(student_ref, teacher_ref, near_ref, term_in, ahead_out, term_ref):
    rows = term_ref.shape[0]
    images = (student_ref[...], *unpacked(teacher_ref, rows))
    grad, folded, term = block(images, unpacked(near_ref, rows))
    term_ref[...] = (term_in[...] + term).astype(term_ref.dtype)
    put(ahead_out, 0, grad.astype(BF16))
    loss = loss_row(folded)
    high = loss.astype(BF16).astype(F32)
    ahead_out[ahead_out.shape[0] - EXTRA :, :] = spread(high, loss - high)


def gather_text(own_ref, second_ref, term_ref):
    term_ref[...] = own_ref[...] + second_ref[...].astype(F32)


def gather_images(own_ref, ahead_ref, sums_ref, loss_ref):
    rows, width = own_ref.shape[0], own_ref.shape[1] - LANES
    sums_ref[...] = own_ref[:, :width] + taken(ahead_ref, 0, rows, width).astype(F32)
    high, low = gathered(ahead_ref, ahead_ref.shape[0] - EXTRA, rows)
    loss_ref[...] = loss_row(own_ref[:, width:]) + high + low


def finish_images(sums_in, loss_in, other_ref, grad_ref, loss_ref, done_ref):
    rows, width = grad_ref.shape
    scale = SOFTMAX_TEMP_VALUE / float(width) ** 0.5
    grad_ref[...] = (sums_in[...] + other_ref[:, :width]) * scale
    loss = loss_in[...] + loss_row(other_ref[:, width:])
    loss_ref[...] = (loss / float(WINDOW * rows)).reshape(rows)
    done_ref[...] = jnp.zeros_like(done_ref)


def finish_text(own_ref, near_ref, out_ref):
    scale = SOFTMAX_TEMP_VALUE / float(out_ref.shape[1]) ** 0.5
    out_ref[...] = (own_ref[...] + near_ref[...].astype(F32)) * scale


def shards(student_image_vectors, teacher_emb, text_emb, species):
    rows, width = text_emb.shape
    dot = 2 * rows * rows * width

    def spec(n, m, dtype):
        return jax.ShapeDtypeStruct((n, m), dtype)

    sums = spec(rows, width + LANES, F32)
    term = spec(rows, width, F32)
    sent = spec(rows, width, BF16)
    packed = spec(rows * width // LANES + EXTRA, LANES, BF16)
    ahead_student = back(student_image_vectors)
    (token,) = call(first_token, [spec(8, LANES, F32)], 64 * dot)
    (text,) = call(pack_text, [packed], 0, text_emb, species, after=(token,))
    second = onward(text)
    images, teacher, text_again = call(
        pack_images,
        [spec(2 * rows * width // LANES + EXTRA, LANES, BF16), packed, packed],
        0,
        student_image_vectors,
        teacher_emb,
        species,
        text,
    )
    near = across(text_again)
    other = within(images)
    ahead_teacher = back(teacher)
    own_sum, own_term = call(
        own_first, [sums, term], 64 * dot, images, text, after=(ahead_student,)
    )
    other_sum, own_term = call(other_first, [sums, term], 16 * dot, other, text, own_term)
    own_sum, other_sum, second_term = call(
        both, [sums, sums, sent], 16 * dot, images, other, second, own_sum, other_sum
    )
    second_back = back(second_term)
    own_sum, other_sum, near_term = call(
        both, [sums, sums, term], 0 * dot, images, other, near, own_sum, other_sum
    )
    ahead_sum, near_term = call(
        ahead_near, [packed, sent], 0 * dot, ahead_student, ahead_teacher, near, near_term
    )
    ahead_back = onward(ahead_sum)
    near_back = across(near_term)
    other_back = within(other_sum)
    (own_term,) = call(gather_text, [term], 128 * dot, own_term, second_back)
    own_sum, loss = call(
        gather_images, [term, spec(1, rows, F32)], 64 * dot, own_sum, ahead_back, after=(own_term,)
    )
    grad_student, loss, done = call(
        finish_images,
        [term, jax.ShapeDtypeStruct((rows,), F32), spec(8, LANES, F32)],
        0,
        own_sum,
        loss,
        other_back,
    )
    (grad_text,) = call(finish_text, [term], 0, own_term, near_back, after=(done,))
    return grad_student, grad_text, loss


def solution(mesh):
    return jax.shard_map(
        shards,
        mesh=mesh,
        in_specs=(P("dp", None), P("dp", None), P("dp", None), P("dp")),
        out_specs=(P("dp", None), P("dp", None), P("dp")),
        check_vma=False,
    )
```

```python
import jax
import jax.numpy as jnp
from jax import lax
from jax.experimental import pallas as pl
from jax.experimental.pallas import tpu as pltpu
from jax.sharding import PartitionSpec as P

SOFTMAX_TEMP_VALUE = 4.0
LOGIT_BIAS = -3.0
WINDOW = 7
DIGIT = 32.0
LANES = 128
EXTRA = 16

BF16 = jnp.bfloat16
F32 = jnp.float32


def moved(value, even, odd):
    length = lax.axis_size("dp")
    return lax.ppermute(
        value, "dp", [(i, (i + (odd if i % 2 else even)) % length) for i in range(length)]
    )


def within(value):
    return moved(value, 1, -1)


def across(value):
    return moved(value, -1, 1)


def onward(value):
    return moved(value, 2, -2)


def back(value):
    return moved(value, -2, 2)


def call(body, out_shape, flops, *args, after=()):
    count = len(args)

    def ordered(*refs):
        body(*refs[:count], *refs[count + len(after) :])

    in_bytes = sum(a.size * a.dtype.itemsize for a in args)
    out_bytes = sum(o.size * o.dtype.itemsize for o in out_shape)
    return pl.pallas_call(
        ordered,
        out_shape=out_shape,
        in_specs=[pl.BlockSpec(memory_space=pltpu.VMEM)] * count
        + [pl.BlockSpec(memory_space=pl.ANY)] * len(after),
        out_specs=[pl.BlockSpec(memory_space=pltpu.VMEM)] * len(out_shape),
        compiler_params=pltpu.CompilerParams(vmem_limit_bytes=40 * 1024 * 1024),
        cost_estimate=pl.CostEstimate(
            flops=flops, bytes_accessed=in_bytes + out_bytes, transcendentals=0
        ),
    )(*args, *after)


def spread(first, second):
    tiles = [
        row[:, k : k + LANES] for row in (first, second) for k in range(0, row.shape[1], LANES)
    ]
    place = lax.broadcasted_iota(jnp.int32, (EXTRA, LANES), 0)
    out = jnp.zeros((EXTRA, LANES), F32)
    for k, tile in enumerate(tiles):
        out = jnp.where(place == k, tile, out)
    return out.astype(BF16)


def gathered(ref, start, rows):
    tiles = ref[start:, :].astype(F32)
    count = rows // LANES
    first = jnp.concatenate([tiles[k : k + 1, :] for k in range(count)], axis=1)
    second = jnp.concatenate([tiles[k : k + 1, :] for k in range(count, 2 * count)], axis=1)
    return first, second


def digits(species):
    ids = species.reshape(1, species.shape[0]).astype(F32)
    high = jnp.floor(ids / DIGIT)
    return spread(high, ids - high * DIGIT)


def ids_of(ref, rows):
    high, low = gathered(ref, ref.shape[0] - EXTRA, rows)
    return high * DIGIT + low


def put(out_ref, start, value):
    rows = value.shape[0]
    for k in range(value.shape[1] // LANES):
        out_ref[start + k * rows : start + (k + 1) * rows, :] = value[:, k * LANES : (k + 1) * LANES]


def taken(ref, start, rows, width):
    count = width // LANES
    tiles = [ref[start + k * rows : start + (k + 1) * rows, :] for k in range(count)]
    return jnp.concatenate(tiles, axis=1)


def pack_text(text_ref, species_ref, out_ref):
    put(out_ref, 0, text_ref[...])
    out_ref[out_ref.shape[0] - EXTRA :, :] = digits(species_ref[...])


def first_token(out_ref):
    out_ref[...] = jnp.zeros_like(out_ref)


def pack_images(student_ref, teacher_ref, species_ref, text_ref, out_ref, teacher_out, text_out):
    text_out[...] = text_ref[...]
    rows, width = student_ref.shape
    ids = digits(species_ref[...])
    put(out_ref, 0, student_ref[...])
    put(out_ref, rows * width // LANES, teacher_ref[...])
    out_ref[out_ref.shape[0] - EXTRA :, :] = ids
    put(teacher_out, 0, teacher_ref[...])
    teacher_out[teacher_out.shape[0] - EXTRA :, :] = ids


def pair(student, teacher, ids, text, text_ids):
    rows, width = student.shape
    half_scale = 0.5 * SOFTMAX_TEMP_VALUE / float(width) ** 0.5
    contract = (((1,), (1,)), ((), ()))
    half_z = (
        lax.dot_general(student, text, contract, preferred_element_type=F32) * half_scale
        + 0.5 * LOGIT_BIAS
    )
    half_w = (
        lax.dot_general(teacher, text, contract, preferred_element_type=F32) * half_scale
        + 0.5 * LOGIT_BIAS
    )
    column = jnp.transpose(jnp.broadcast_to(ids, (LANES, rows)))
    column = jnp.concatenate([column] * (rows // LANES), axis=1)
    shift = jnp.where(column == text_ids, 0.75, 0.25)
    target = 0.25 * jnp.tanh(half_w) + shift
    tanh_z = jnp.tanh(half_z)
    slope = (0.5 * tanh_z + 0.5) - target
    z = half_z + half_z
    loss = (jnp.maximum(z, 0.0) - target * z) - jnp.log(0.5 * jnp.abs(tanh_z) + 0.5)
    folded = sum(loss[:, k : k + LANES] for k in range(0, rows, LANES))
    return slope.astype(BF16), folded


def text_term(slope, student):
    return lax.dot_general(slope, student, (((0,), (0,)), ((), ())), preferred_element_type=F32)


def unpacked(ref, rows):
    width = (ref.shape[0] - EXTRA) * LANES // rows
    return taken(ref, 0, rows, width), ids_of(ref, rows)


def both_images(ref, rows):
    size = (ref.shape[0] - EXTRA) // 2
    width = size * LANES // rows
    return taken(ref, 0, rows, width), taken(ref, size, rows, width), ids_of(ref, rows)


def block(images, texts):
    student, teacher, ids = images
    slope, folded = pair(student, teacher, ids, *texts)
    grad = jnp.dot(slope, texts[0], preferred_element_type=F32)
    return grad, folded, text_term(slope, student)


def two_blocks(images, texts, sums_in, sums_out):
    rows, width = texts[0].shape
    pairs = [pair(student, teacher, ids, *texts) for student, teacher, ids in images]
    slope = jnp.concatenate([slope for slope, _ in pairs], axis=0)
    grad = jnp.dot(slope, texts[0], preferred_element_type=F32)
    for k, (was, out) in enumerate(zip(sums_in, sums_out)):
        out[:, :width] = was[:, :width] + grad[k * rows : (k + 1) * rows, :]
        out[:, width:] = was[:, width:] + pairs[k][1]
    return text_term(slope, jnp.concatenate([student for student, _, _ in images], axis=0))


def own_first(own_ref, text_ref, sums_ref, term_ref):
    rows, width = term_ref.shape
    images = both_images(own_ref, rows)
    sums_ref[:, :width], sums_ref[:, width:], term_ref[...] = block(images, unpacked(text_ref, rows))


def other_first(other_ref, text_ref, term_in, sums_ref, term_ref):
    rows, width = term_ref.shape
    images = both_images(other_ref, rows)
    sums_ref[:, :width], sums_ref[:, width:], term = block(images, unpacked(text_ref, rows))
    term_ref[...] = term_in[...] + term


def both(own_ref, other_ref, text_ref, own_in, other_in, own_out, other_out, term_ref):
    rows = term_ref.shape[0]
    images = [both_images(ref, rows) for ref in (own_ref, other_ref)]
    sums_in, sums_out = (own_in, other_in), (own_out, other_out)
    term = two_blocks(images, unpacked(text_ref, rows), sums_in, sums_out)
    term_ref[...] = term.astype(term_ref.dtype)


def loss_row(folded):
    return jnp.sum(jnp.transpose(folded), axis=0, keepdims=True)


def ahead_near(student_ref, teacher_ref, near_ref, term_in, ahead_out, term_ref):
    rows = term_ref.shape[0]
    images = (student_ref[...], *unpacked(teacher_ref, rows))
    grad, folded, term = block(images, unpacked(near_ref, rows))
    term_ref[...] = (term_in[...] + term).astype(term_ref.dtype)
    put(ahead_out, 0, grad.astype(BF16))
    loss = loss_row(folded)
    high = loss.astype(BF16).astype(F32)
    ahead_out[ahead_out.shape[0] - EXTRA :, :] = spread(high, loss - high)


def gather_text(own_ref, second_ref, term_ref):
    term_ref[...] = own_ref[...] + second_ref[...].astype(F32)


def gather_images(own_ref, ahead_ref, sums_ref, loss_ref):
    rows, width = own_ref.shape[0], own_ref.shape[1] - LANES
    sums_ref[...] = own_ref[:, :width] + taken(ahead_ref, 0, rows, width).astype(F32)
    high, low = gathered(ahead_ref, ahead_ref.shape[0] - EXTRA, rows)
    loss_ref[...] = loss_row(own_ref[:, width:]) + high + low


def finish_images(sums_in, loss_in, other_ref, grad_ref, loss_ref, done_ref):
    rows, width = grad_ref.shape
    scale = SOFTMAX_TEMP_VALUE / float(width) ** 0.5
    grad_ref[...] = (sums_in[...] + other_ref[:, :width]) * scale
    loss = loss_in[...] + loss_row(other_ref[:, width:])
    loss_ref[...] = (loss / float(WINDOW * rows)).reshape(rows)
    done_ref[...] = jnp.zeros_like(done_ref)


def finish_text(own_ref, near_ref, out_ref):
    scale = SOFTMAX_TEMP_VALUE / float(out_ref.shape[1]) ** 0.5
    out_ref[...] = (own_ref[...] + near_ref[...].astype(F32)) * scale


def shards(student_image_vectors, teacher_emb, text_emb, species):
    rows, width = text_emb.shape
    dot = 2 * rows * rows * width

    def spec(n, m, dtype):
        return jax.ShapeDtypeStruct((n, m), dtype)

    sums = spec(rows, width + LANES, F32)
    term = spec(rows, width, F32)
    sent = spec(rows, width, BF16)
    packed = spec(rows * width // LANES + EXTRA, LANES, BF16)
    ahead_student = back(student_image_vectors)
    (token,) = call(first_token, [spec(8, LANES, F32)], 64 * dot)
    (text,) = call(pack_text, [packed], 0, text_emb, species, after=(token,))
    second = onward(text)
    images, teacher, text_again = call(
        pack_images,
        [spec(2 * rows * width // LANES + EXTRA, LANES, BF16), packed, packed],
        0,
        student_image_vectors,
        teacher_emb,
        species,
        text,
    )
    near = across(text_again)
    other = within(images)
    ahead_teacher = back(teacher)
    own_sum, own_term = call(own_first, [sums, term], 64 * dot, images, text)
    other_sum, own_term = call(
        other_first, [sums, term], 16 * dot, other, text, own_term, after=(ahead_student,)
    )
    own_sum, other_sum, second_term = call(
        both, [sums, sums, sent], 16 * dot, images, other, second, own_sum, other_sum
    )
    second_back = back(second_term)
    own_sum, other_sum, near_term = call(
        both, [sums, sums, term], 0 * dot, images, other, near, own_sum, other_sum
    )
    ahead_sum, near_term = call(
        ahead_near, [packed, sent], 0 * dot, ahead_student, ahead_teacher, near, near_term
    )
    ahead_back = onward(ahead_sum)
    near_back = across(near_term)
    other_back = within(other_sum)
    (own_term,) = call(gather_text, [term], 128 * dot, own_term, second_back)
    own_sum, loss = call(
        gather_images, [term, spec(1, rows, F32)], 64 * dot, own_sum, ahead_back, after=(own_term,)
    )
    grad_student, loss, done = call(
        finish_images,
        [term, jax.ShapeDtypeStruct((rows,), F32), spec(8, LANES, F32)],
        0,
        own_sum,
        loss,
        other_back,
    )
    (grad_text,) = call(finish_text, [term], 0, own_term, near_back, after=(done,))
    return grad_student, grad_text, loss


def solution(mesh):
    return jax.shard_map(
        shards,
        mesh=mesh,
        in_specs=(P("dp", None), P("dp", None), P("dp", None), P("dp")),
        out_specs=(P("dp", None), P("dp", None), P("dp")),
        check_vma=False,
    )
```
